32 devices in a mesh: section: 2 (over y), fsdp: 16 (over z, x, core).
Axes of the slice: x: 2, y: 2, z: 4, core: 2. Of those that a mesh axis runs over, the one named last changes fastest.
Arguments:
- clips: bfloat16 [64, 4, 8, 4, 256], P('fsdp'), may hold values from -30 to 30
- plan: int32 [16, 4], P('fsdp'), may hold values from 0 to 3, each once within a row
- gains: float32 [2, 256], P('section'), may hold values from 0.1 to 1.9
- weights: bfloat16 [2, 6912, 256], P('section', 'fsdp'), may hold values from -0.078125 to 0.078125
- cotangent: bfloat16 [64, 4, 8, 4, 256], P('fsdp'), may hold values from -6 to 6
Outputs:
- acts: bfloat16 [2, 64, 4, 8, 4, 256], P('section', 'fsdp')
- grad_in: bfloat16 [2, 64, 4, 8, 4, 256], P('section', 'fsdp')
- weight_grad: float32 [2, 6912, 256], P('section', 'fsdp')
The draws below stay inside these ranges and needn't reach their ends.
Inputs may be any that keep to these rules, and one draw needn't show every extreme that they name: Each row of plan names every clip of its group once.
All inputs are finite; a program needn't handle non-finite values.
Results may differ from the reference program's by a relative error of at most 0.012.
The reference program's roundings to bfloat16 on the way (of `ordered` and `active`) count: a program that leaves them out, or rounds other values in their place, can miss the bound.
Values may be sent and summed in bfloat16 or wider, within the bound.
No kernel may reach another device: no remote copies, remote signals or barrier semaphores. Data moves between devices by JAX's collectives and lax.ppermute only.
A program may use at most 64 MiB of HBM per device.

```python
import math
import jax
import jax.numpy as jnp
from jax import lax

C = 256
MICRO = 4
FRAMES = 4
HEIGHT = 8
WIDTH = 4
KC = 6912
VOXELS = 128
CLIPS = 64
N_FSDP = 16


def draw_clips(key, part):
    key = jax.random.fold_in(key, 11)
    normal_key, scale_key = jax.random.split(key, 2)
    values = jax.random.normal(normal_key, (CLIPS, FRAMES, HEIGHT, WIDTH, C), jnp.float32)
    scales = jnp.exp(jax.random.uniform(scale_key, (CLIPS, FRAMES, HEIGHT, WIDTH, 1), jnp.float32, math.log(0.5), math.log(5.0)))
    return jnp.clip(values * scales, -30.0, 30.0).astype(jnp.bfloat16)


def level_of(key, shape, cuts, low, top_value):
    factor_of = 1.0
    for axis_at, shards_of in cuts:
        draws = jax.random.uniform(jax.random.fold_in(jax.random.fold_in(key, 6), axis_at), (shards_of,), jnp.float32, low / len(cuts), top_value / len(cuts))
        factor_of = factor_of * jnp.repeat(jnp.exp(draws), shape[axis_at] // shards_of).reshape((-1,) + (1,) * (len(shape) - 1 - axis_at))
    return factor_of


def normal_values(rng, extent, scale, reach, cuts=(), kind=jnp.bfloat16):
    values = jax.random.normal(rng, extent, jnp.float32) * scale
    if len(cuts) > 0:
        values = level_of(rng, extent, cuts, -0.22, 0.18) * values
    return jnp.clip(values, min=-reach, max=reach).astype(kind)


def setup_inputs(seed: int = 0) -> dict:
    streams_of = jax.random.split(jax.random.key(seed), 6)
    return {
        "clips": draw_clips(jax.random.fold_in(streams_of[5], 71), 0),
        "plan": jax.vmap(lambda own: jax.random.permutation(own, MICRO))(jax.random.split(streams_of[1], N_FSDP)).reshape((N_FSDP, MICRO)).astype(jnp.int32),
        "gains": jnp.clip(1.0 + 0.18 * jax.random.normal(streams_of[2], (2, C), jnp.float32), 0.1, 1.9),
        "weights": normal_values(streams_of[3], (2, KC, C), KC ** -0.5, 0.078125, ((0, 2), (1, 16))),
        "cotangent": normal_values(streams_of[4], (CLIPS, FRAMES, HEIGHT, WIDTH, C), 1.0, 6.0, ((0, 16),)),
    }


EPSILON = 1e-06

def unfold(volume):
    frames, height, breadth, channels = volume.shape
    padded = jnp.pad(volume, ((1, 1), (1, 1), (1, 1), (0, 0)))
    pieces = []
    for along_t in range(3):
        for along_h in range(3):
            for along_w in range(3):
                pieces.append(padded[along_t:along_t + frames, along_h:along_h + height, along_w:along_w + breadth, :])
    return jnp.concatenate(pieces, axis=-1).reshape(frames * height * breadth, 27 * channels)

def normalize(volume, gain_row):
    values = volume.astype(jnp.float32)
    inverse = lax.rsqrt(lax.optimization_barrier(jnp.mean(values * values, axis=-1, keepdims=True)) + EPSILON)
    normed = values * inverse * gain_row
    return (values, inverse, normed)

def active_columns(volume, gain_row):
    values, inverse, normed = normalize(volume, gain_row)
    return unfold(jnp.maximum(normed, 0.0).astype(jnp.bfloat16))

def forward_block(volume, gain_row, full_weight):
    values, inverse, normed = normalize(volume, gain_row)
    active = jnp.maximum(normed, 0.0).astype(jnp.bfloat16)
    branch = jnp.dot(unfold(active), full_weight, preferred_element_type=jnp.float32)
    return (values + branch.reshape(values.shape)).astype(jnp.bfloat16)

def backward_block(volume, upstream, gain_row, reversed_weight):
    values, inverse, normed = normalize(volume, gain_row)
    channels = values.shape[-1]
    columns = unfold(upstream).reshape(-1, 27, channels)
    spread = lax.dot_general(columns, reversed_weight, (((1, 2), (0, 2)), ((), ())), preferred_element_type=jnp.float32)
    spread = spread.reshape(values.shape)
    scaled = gain_row * jnp.where(normed > 0.0, spread, 0.0)
    mixing = lax.optimization_barrier(jnp.mean(values * scaled, axis=-1, keepdims=True))
    grad_input = upstream.astype(jnp.float32) + inverse * scaled - values * inverse ** 3 * mixing
    return grad_input.astype(jnp.bfloat16)

def weight_term(volume, upstream, gain_row):
    columns = active_columns(volume, gain_row)
    flattened = upstream.reshape(-1, upstream.shape[-1])
    return lax.dot_general(columns, flattened, (((0,), (0,)), ((), ())), preferred_element_type=jnp.float32)

def run_forward(volumes, gain_row, full_weight):
    return lax.map(lambda clip_in: forward_block(clip_in, gain_row, full_weight), volumes)

def run_backward(volumes, upstreams, gain_row, full_weight):
    channels = full_weight.shape[1]
    reversed_weight = full_weight.reshape(27, channels, channels)[::-1]

    def accumulate(running, paired):
        grad_input = backward_block(paired[0], paired[1], gain_row, reversed_weight)
        return (running + weight_term(paired[0], paired[1], gain_row), grad_input)
    starting = jnp.zeros(full_weight.shape, jnp.float32)
    summed, grads = lax.scan(accumulate, starting, (volumes, upstreams))
    return (summed, grads)

def reference(clips, plan, gains, weights, cotangent):
    position_base = (jnp.arange(N_FSDP, dtype=jnp.int32)[:, None] * MICRO + plan).reshape(-1).astype(jnp.int32)
    ordered = jnp.take(clips, position_base, axis=0)
    hidden = run_forward(ordered, gains[0], weights[0])
    last_out = run_forward(hidden, gains[1], weights[1])
    summed_one, grads_one = run_backward(hidden, cotangent, gains[1], weights[1])
    summed_zero, grads_zero = run_backward(ordered, grads_one, gains[0], weights[0])
    factor = 1.0 / math.sqrt(N_FSDP * MICRO * VOXELS)
    return (jnp.stack([hidden, last_out]), jnp.stack([grads_zero, grads_one]), jnp.stack([summed_zero, summed_one]) * factor)
```

```python
import functools
import math

import jax
import jax.numpy as jnp
from jax import lax
from jax.experimental import pallas as pl
from jax.experimental.pallas import tpu as pltpu
from jax.sharding import PartitionSpec as P

EPSILON = 1e-06
ROW_TILE = 16
VMEM_LIMIT = 48 * 1024 * 1024


def normalize(values, gain_row):
    inverse = lax.rsqrt(jnp.mean(values * values, axis=-1, keepdims=True) + EPSILON)
    return inverse, values * inverse * gain_row


def activate(values, gain_row):
    inverse, normed = normalize(values, gain_row)
    return jnp.maximum(normed, 0.0).astype(jnp.bfloat16)


def back(values, upstream, spread, gain_row):
    inverse, normed = normalize(values, gain_row)
    scaled = gain_row * jnp.where(normed > 0.0, spread, 0.0)
    mixing = jnp.mean(values * scaled, axis=-1, keepdims=True)
    return upstream + inverse * scaled - values * (inverse * inverse * inverse) * mixing


def fill_columns(cols_ref, values, dims):
    micro, frames, height, width, channels = dims
    plane = height * width
    voxels = frames * plane
    total = micro * voxels
    row = lax.broadcasted_iota(jnp.int32, (plane, channels), 0)
    across = row % width
    down = row // width
    zero = jnp.zeros((micro, plane, cols_ref.shape[2]), jnp.bfloat16)
    cols_ref[:, :plane, :] = zero
    cols_ref[:, plane + voxels :, :] = zero

    def masked(rolled, inside):
        kept = rolled.reshape(total // plane, plane, channels) * inside.astype(jnp.float32)[None]
        return kept.reshape(total, channels)

    for by_w in (-1, 0, 1):
        if by_w == 0:
            along = values
        else:
            inside = (across + by_w >= 0) & (across + by_w < width)
            along = masked(pltpu.roll(values, (-by_w) % total, 0), inside)
        for by_h in (-1, 0, 1):
            if by_h == 0:
                moved = along
            else:
                inside = (down + by_h >= 0) & (down + by_h < height)
                moved = masked(pltpu.roll(along, (-by_h * width) % total, 0), inside)
            j = 3 * (by_h + 1) + by_w + 1
            cols_ref[:, plane : plane + voxels, j * channels : (j + 1) * channels] = moved.astype(
                jnp.bfloat16
            ).reshape(micro, voxels, channels)


def frame_columns(cols_ref, by_t, dims, begin, end):
    micro, frames, height, width, channels = dims
    plane = height * width
    voxels = frames * plane
    start = plane * (by_t + 1)
    return cols_ref[:, start : start + voxels, begin:end].reshape(micro * voxels, end - begin)


def convolve(cols_ref, weight_ref, dims):
    channels = dims[4]
    total = None
    for by_t in (-1, 0, 1):
        first = 9 * (by_t + 1) * channels
        term = jnp.dot(
            frame_columns(cols_ref, by_t, dims, 0, 9 * channels),
            weight_ref[first : first + 9 * channels, :],
            preferred_element_type=jnp.float32,
        )
        total = term if total is None else total + term
    return total


def convolve_back(cols_ref, weight_ref, dims):
    channels = dims[4]
    total = None
    for by_t in (-1, 0, 1):
        for j in range(9):
            k = 26 - (9 * (by_t + 1) + j)
            term = lax.dot_general(
                frame_columns(cols_ref, by_t, dims, j * channels, (j + 1) * channels),
                weight_ref[k * channels : (k + 1) * channels, :],
                (((1,), (1,)), ((), ())),
                preferred_element_type=jnp.float32,
            )
            total = term if total is None else total + term
    return total


def gather_copies(place_ref, pieces, weight_ref, sems):
    copies = []
    for at, piece in enumerate(pieces):
        rows = piece.shape[0]
        start = place_ref[at] if len(pieces) > 1 else 0
        if len(pieces) > 1:
            start = pl.multiple_of(start, ROW_TILE)
        copies.append(pltpu.make_async_copy(piece, weight_ref.at[pl.ds(start, rows)], sems.at[at]))
    return copies


def take_clips(plan_ref, clips_ref, dims):
    micro, channels = dims[0], dims[4]
    picked = [clips_ref[plan_ref[m]] for m in range(micro)]
    return jnp.concatenate(picked, axis=0).astype(jnp.float32)


def first_kernel(dims, count, flag_ref, plan_ref, place_ref, clips_ref, cotangent_ref, gain_ref, *rest):
    pieces, (out_ref, weight_ref, cols_ref, sems) = rest[:count], rest[count:]
    copies = gather_copies(place_ref, pieces, weight_ref, sems)
    for copy in copies:
        copy.start()
    total = dims[0] * dims[1] * dims[2] * dims[3]
    leading = flag_ref[0] == 0
    ordered = take_clips(plan_ref, clips_ref, dims)
    upstream = cotangent_ref[...].reshape(total, dims[4]).astype(jnp.float32)
    active = activate(ordered, gain_ref[...]).astype(jnp.float32)
    fill_columns(cols_ref, jnp.where(leading, active, upstream), dims)
    for copy in copies:
        copy.wait()

    @pl.when(leading)
    def _():
        branch = convolve(cols_ref, weight_ref, dims)
        out_ref[...] = (take_clips(plan_ref, clips_ref, dims) + branch).astype(jnp.bfloat16)

    @pl.when(jnp.logical_not(leading))
    def _():
        out_ref[...] = convolve_back(cols_ref, weight_ref, dims).astype(jnp.bfloat16)


def second_kernel(dims, count, flag_ref, plan_ref, place_ref, clips_ref, cotangent_ref, gain_ref, last_gain_ref,
                  mine_ref, theirs_ref, *rest):
    grad_ref, pieces = rest[0], rest[1 : 1 + count]
    turned_ref, cols_ref, sums_ref, sems = rest[1 + count :]
    channels = dims[4]
    total = dims[0] * dims[1] * dims[2] * dims[3]
    leading = flag_ref[0] == 0
    mine = mine_ref[...].astype(jnp.float32)
    theirs = theirs_ref[...].astype(jnp.float32)
    hidden = jnp.where(leading, mine, theirs)
    spread = jnp.where(leading, theirs, mine)
    cotangent = cotangent_ref[...].reshape(total, channels).astype(jnp.float32)
    upstream = back(hidden, cotangent, spread, last_gain_ref[...]).astype(jnp.bfloat16)
    grad_ref[...] = upstream
    ordered = take_clips(plan_ref, clips_ref, dims)
    active = activate(jnp.where(leading, ordered, hidden), gain_ref[...])
    turned_ref[...] = active.T
    fill_columns(cols_ref, jnp.where(leading, upstream.astype(jnp.float32), cotangent), dims)
    for by_t in (-1, 0, 1):
        for j in range(9):
            k = 26 - (9 * (by_t + 1) + j)
            sums_ref[k * channels : (k + 1) * channels, :] = jnp.dot(
                turned_ref[...],
                frame_columns(cols_ref, by_t, dims, j * channels, (j + 1) * channels),
                preferred_element_type=jnp.float32,
            ).astype(jnp.bfloat16)
    copies = []
    at = 0
    for number, piece in enumerate(pieces):
        rows = piece.shape[-2]
        if len(piece.shape) == 2:
            copies.append(pltpu.make_async_copy(sums_ref, piece, sems.at[0]))
        else:
            for inner in range(piece.shape[0]):
                start = pl.multiple_of(place_ref[at], ROW_TILE)
                copies.append(
                    pltpu.make_async_copy(sums_ref.at[pl.ds(start, rows)], piece.at[inner], sems.at[at])
                )
                at += 1
    for copy in copies:
        copy.start()
    for copy in copies:
        copy.wait()


def third_kernel(dims, count, flag_ref, plan_ref, place_ref, clips_ref, gain_ref, mine_ref, theirs_ref, grad_ref,
                 *rest):
    pieces, (acts_ref, grads_ref, weight_ref, cols_ref, sems) = rest[:count], rest[count:]
    copies = gather_copies(place_ref, pieces, weight_ref, sems)
    for copy in copies:
        copy.start()
    leading = flag_ref[0] == 0
    gain_row = gain_ref[...]

    @pl.when(leading)
    def _():
        fill_columns(cols_ref, grad_ref[...].astype(jnp.float32), dims)

    @pl.when(jnp.logical_not(leading))
    def _():
        hidden = theirs_ref[...].astype(jnp.float32)
        fill_columns(cols_ref, activate(hidden, gain_row).astype(jnp.float32), dims)

    for copy in copies:
        copy.wait()

    @pl.when(leading)
    def _():
        spread = convolve_back(cols_ref, weight_ref, dims)
        ordered = take_clips(plan_ref, clips_ref, dims)
        upstream = grad_ref[...].astype(jnp.float32)
        grads_ref[...] = back(ordered, upstream, spread, gain_row).astype(jnp.bfloat16)
        acts_ref[...] = mine_ref[...]

    @pl.when(jnp.logical_not(leading))
    def _():
        branch = convolve(cols_ref, weight_ref, dims)
        acts_ref[...] = (theirs_ref[...].astype(jnp.float32) + branch).astype(jnp.bfloat16)
        grads_ref[...] = grad_ref[...]


def swap(value, axis, by):
    return lax.ppermute(value, axis, [(i, i ^ by) for i in range(lax.axis_size(axis))])


def plain_sum(left, right):
    return left.astype(jnp.float32) + right.astype(jnp.float32)


def on_device(clips, plan, gains, weights, cotangent):
    section = lax.axis_index("section")
    peers = lax.axis_size("fsdp")
    place = lax.axis_index("fsdp")
    micro, frames, height, width, channels = clips.shape
    dims = clips.shape
    voxels = frames * height * width
    total = micro * voxels
    rows = weights.shape[1]
    all_rows = rows * peers
    factor = 1.0 / math.sqrt(peers * total)
    flag = section.astype(jnp.int32).reshape(1)
    order = plan[0]
    flat_clips = clips.reshape(micro, voxels, channels)
    flat_cotangent = cotangent.reshape(micro, voxels, channels)
    other_gain = swap(gains, "section", 1)
    last_gain = jnp.where(section == 0, other_gain, gains)
    split = peers == 16 and rows % ROW_TILE == 0

    own = weights[0]
    if split:
        far = {0: own}
        for by in (4, 8, 12):
            far[by] = swap(own, "fsdp", by)
        near = {}
        for by in (0, 4, 8, 12):
            near[by] = far[by]
            near[by + 2] = swap(far[by], "fsdp", 2)
        held = dict(near)
        for by in near:
            held[by + 1] = swap(near[by], "fsdp", 1)
        offsets = sorted(held)
        pieces = [held[by] for by in offsets]
        places = jnp.stack([(place ^ by) * rows for by in offsets]).astype(jnp.int32)
    else:
        pieces = [lax.all_gather(own, "fsdp", axis=0, tiled=True)]
        places = jnp.zeros((1,), jnp.int32)

    count = len(pieces)
    smem = pl.BlockSpec(memory_space=pltpu.SMEM)
    vmem = pl.BlockSpec(memory_space=pltpu.VMEM)
    anywhere = pl.BlockSpec(memory_space=pl.ANY)
    weight_scratch = pltpu.VMEM((all_rows, channels), jnp.bfloat16)
    cols_scratch = pltpu.VMEM((micro, voxels + 2 * height * width, 9 * channels), jnp.bfloat16)
    volume = jax.ShapeDtypeStruct((total, channels), jnp.bfloat16)
    flops = 2 * total * all_rows * channels
    params = pltpu.CompilerParams(vmem_limit_bytes=VMEM_LIMIT)
    cost = pl.CostEstimate(flops=flops, bytes_accessed=2 * all_rows * channels, transcendentals=0)

    mine = pl.pallas_call(
        functools.partial(first_kernel, dims, count),
        out_shape=volume,
        in_specs=[smem] * 3 + [vmem] * 3 + [anywhere] * count,
        out_specs=vmem,
        scratch_shapes=[weight_scratch, cols_scratch, pltpu.SemaphoreType.DMA((count,))],
        compiler_params=params,
        cost_estimate=cost,
    )(flag, order, places, flat_clips, flat_cotangent, gains, *pieces)

    theirs = swap(mine, "section", 1)

    if split:
        shapes = [jax.ShapeDtypeStruct((2, rows, channels), jnp.bfloat16)] * 8
        outward = []
        for by in (0, 4, 8, 12):
            outward += [by, by + 2, by + 1, by + 3]
        out_places = jnp.stack([(place ^ by) * rows for by in outward]).astype(jnp.int32)
    else:
        shapes = [jax.ShapeDtypeStruct((all_rows, channels), jnp.bfloat16)]
        out_places = places
    grad, *partial_sums = pl.pallas_call(
        functools.partial(second_kernel, dims, len(shapes)),
        out_shape=[volume] + shapes,
        in_specs=[smem] * 3 + [vmem] * 6,
        out_specs=[vmem] + [anywhere] * len(shapes),
        scratch_shapes=[
            pltpu.VMEM((channels, total), jnp.bfloat16),
            cols_scratch,
            weight_scratch,
            pltpu.SemaphoreType.DMA((2 * len(shapes),)),
        ],
        compiler_params=params,
        cost_estimate=cost,
    )(flag, order, out_places, flat_clips, flat_cotangent, gains, last_gain, mine, theirs)

    if split:
        arrived = []
        for at in (3, 2, 1, 0):
            kept, sent = partial_sums[2 * at], partial_sums[2 * at + 1]
            both = plain_sum(kept, swap(sent, "fsdp", 1))
            across = swap(both[1].astype(jnp.bfloat16), "fsdp", 2)
            chip_pair = both[0] + across.astype(jnp.float32)
            if at:
                arrived.append(swap(chip_pair.astype(jnp.bfloat16), "fsdp", 4 * at).astype(jnp.float32))
            else:
                arrived.append(chip_pair)
        weight_grad = sum(arrived[1:], arrived[0]) * factor
    else:
        summed = partial_sums[0].astype(jnp.float32)
        weight_grad = lax.psum_scatter(summed, "fsdp", scatter_dimension=0, tiled=True) * factor

    acts, grads = pl.pallas_call(
        functools.partial(third_kernel, dims, count),
        out_shape=[volume, volume],
        in_specs=[smem] * 3 + [vmem] * 5 + [anywhere] * count,
        out_specs=[vmem, vmem],
        scratch_shapes=[weight_scratch, cols_scratch, pltpu.SemaphoreType.DMA((count,))],
        compiler_params=params,
        cost_estimate=cost,
    )(flag, order, places, flat_clips, gains, mine, theirs, grad, *pieces)
    return (acts.reshape(1, *dims), grads.reshape(1, *dims), weight_grad[None])


def solution(mesh):
    placed = (
        P("fsdp", None, None, None, None),
        P("fsdp", None),
        P("section", None),
        P("section", "fsdp", None),
        P("fsdp", None, None, None, None),
    )
    return jax.shard_map(
        on_device,
        mesh=mesh,
        in_specs=placed,
        out_specs=(
            P("section", "fsdp", None, None, None, None),
            P("section", "fsdp", None, None, None, None),
            P("section", "fsdp", None),
        ),
        check_vma=False,
    )
```

```python
import functools
import math

import jax
import jax.numpy as jnp
from jax import lax
from jax.experimental import pallas as pl
from jax.experimental.pallas import tpu as pltpu
from jax.sharding import PartitionSpec as P

EPSILON = 1e-06
ROW_TILE = 16
VMEM_LIMIT = 20 * 1024 * 1024
LAST_VMEM_LIMIT = 24 * 1024 * 1024


def normalize(values, gain_row):
    inverse = lax.rsqrt(jnp.mean(values * values, axis=-1, keepdims=True) + EPSILON)
    return inverse, values * inverse * gain_row


def activate(values, gain_row):
    inverse, normed = normalize(values, gain_row)
    return jnp.maximum(normed, 0.0).astype(jnp.bfloat16)


def back(values, upstream, spread, gain_row):
    inverse, normed = normalize(values, gain_row)
    scaled = gain_row * jnp.where(normed > 0.0, spread, 0.0)
    mixing = jnp.mean(values * scaled, axis=-1, keepdims=True)
    return upstream + inverse * scaled - values * (inverse * inverse * inverse) * mixing


def fill_columns(cols_ref, values, dims):
    micro, frames, height, width, channels = dims
    plane = height * width
    voxels = frames * plane
    total = micro * voxels
    row = lax.broadcasted_iota(jnp.int32, (plane, channels), 0)
    across = row % width
    down = row // width
    zero = jnp.zeros((micro, plane, cols_ref.shape[2]), jnp.bfloat16)
    cols_ref[:, :plane, :] = zero
    cols_ref[:, plane + voxels :, :] = zero

    def masked(rolled, inside):
        kept = rolled.reshape(total // plane, plane, channels) * inside.astype(jnp.float32)[None]
        return kept.reshape(total, channels)

    for by_w in (-1, 0, 1):
        if by_w == 0:
            along = values
        else:
            inside = (across + by_w >= 0) & (across + by_w < width)
            along = masked(pltpu.roll(values, (-by_w) % total, 0), inside)
        for by_h in (-1, 0, 1):
            if by_h == 0:
                moved = along
            else:
                inside = (down + by_h >= 0) & (down + by_h < height)
                moved = masked(pltpu.roll(along, (-by_h * width) % total, 0), inside)
            j = 3 * (by_h + 1) + by_w + 1
            cols_ref[:, plane : plane + voxels, j * channels : (j + 1) * channels] = moved.astype(
                jnp.bfloat16
            ).reshape(micro, voxels, channels)


def frame_columns(cols_ref, by_t, dims, begin, end):
    micro, frames, height, width, channels = dims
    plane = height * width
    voxels = frames * plane
    start = plane * (by_t + 1)
    return cols_ref[:, start : start + voxels, begin:end].reshape(micro * voxels, end - begin)


def half_pieces(half, dims):
    channels = dims[4]
    middle = channels // 2
    parts = []
    at = 0
    for k in range(14) if half == 0 else range(13, 27):
        low, high = 0, channels
        if k == 13:
            low, high = (0, middle) if half == 0 else (middle, channels)
        parts.append((k, low, high, at))
        at += high - low
    return parts


def half_forward(cols_ref, weight_ref, dims, half):
    channels = dims[4]
    middle = 9 * channels // 2
    if half == 0:
        runs = ((-1, 0, 2 * middle, 0), (0, 0, middle, 2 * middle))
    else:
        runs = ((0, middle, 2 * middle, 0), (1, 0, 2 * middle, middle))
    terms = [
        jnp.dot(
            frame_columns(cols_ref, by_t, dims, begin, end),
            weight_ref[at : at + end - begin, :],
            preferred_element_type=jnp.float32,
        )
        for by_t, begin, end, at in runs
    ]
    return terms[0] + terms[1]


def half_spread(cols_ref, weight_ref, dims, half):
    channels = dims[4]
    total, partial = None, None
    for k, low, high, at in half_pieces(half, dims):
        by_t, j = (26 - k) // 9 - 1, (26 - k) % 9
        term = lax.dot_general(
            frame_columns(cols_ref, by_t, dims, j * channels, (j + 1) * channels),
            weight_ref[at : at + high - low, :],
            (((1,), (1,)), ((), ())),
            preferred_element_type=jnp.float32,
        )
        if high - low < channels:
            partial = term
        else:
            total = term if total is None else total + term
    middle = channels // 2
    if half == 0:
        return jnp.concatenate([total[:, :middle] + partial, total[:, middle:]], axis=1)
    return jnp.concatenate([total[:, :middle], total[:, middle:] + partial], axis=1)


def half_gradient(turned_ref, cols_ref, sums_ref, dims, half):
    channels = dims[4]
    for k, low, high, at in half_pieces(half, dims):
        by_t, j = (26 - k) // 9 - 1, (26 - k) % 9
        sums_ref[at : at + high - low, :] = jnp.dot(
            turned_ref[low:high, :],
            frame_columns(cols_ref, by_t, dims, j * channels, (j + 1) * channels),
            preferred_element_type=jnp.float32,
        ).astype(jnp.bfloat16)


def where_am_i(split):
    place = lax.axis_index("fsdp")
    near = place // (lax.axis_size("fsdp") // 2) if split else 0
    return lax.axis_index("section"), place, near


def lay_pieces(place, pieces, weight_ref):
    if len(pieces) == 1:
        weight_ref[...] = pieces[0][...]
        return
    for by, piece in enumerate(pieces):
        rows = piece.shape[0]
        start = pl.multiple_of(((place ^ by) % len(pieces)) * rows, ROW_TILE)
        weight_ref[pl.ds(start, rows), :] = piece[...]


def take_clips(plan_ref, clips_ref, dims):
    picked = [clips_ref[plan_ref[m]] for m in range(dims[0])]
    return jnp.concatenate(picked, axis=0).astype(jnp.float32)


def on_half(section, half, run):
    for at in (0, 1):
        for part in (0, 1):

            @pl.when((section == at) & (half == part))
            def _(at=at, part=part):
                run(at, part)


def fetch(pairs, sems):
    copies = [pltpu.make_async_copy(source, target, sems.at[at]) for at, (source, target) in enumerate(pairs)]
    for copy in copies:
        copy.start()
    return copies


def wait_all(copies):
    for copy in copies:
        copy.wait()


def prepare_kernel(dims, split, plan_ref, clips_ref, cotangent_ref, gain_ref, early_ref, cols_ref, token_ref):
    section, place, near = where_am_i(split)
    total = dims[0] * dims[1] * dims[2] * dims[3]
    active = activate(take_clips(plan_ref, clips_ref, dims), gain_ref[...])
    upstream = cotangent_ref[...].reshape(total, dims[4]).astype(jnp.float32)
    fill_columns(cols_ref, jnp.where(section == 0, active.astype(jnp.float32), upstream), dims)
    token_ref[...] = jnp.zeros_like(token_ref)


def near_kernel(dims, split, count, cols_ref, early_ref, *rest):
    pieces, (out_ref, token_ref, kept_ref, weight_ref, sems) = rest[:count], rest[count:]
    section, place, near = where_am_i(split)
    lay_pieces(place, pieces, weight_ref)
    copies = fetch([(weight_ref, kept_ref)], sems)

    def run(at, part):
        conv = half_forward if at == 0 else half_spread
        out_ref[...] = conv(cols_ref, weight_ref, dims, part)

    on_half(section, near, run)
    token_ref[...] = early_ref[...]
    wait_all(copies)


def far_kernel(dims, split, count, plan_ref, clips_ref, early_ref, cols_ref, base_ref, *rest):
    pieces, (out_ref, kept_ref, weight_ref, held_ref, sems) = rest[:count], rest[count:]
    section, place, near = where_am_i(split)
    arriving = fetch([(clips_ref, held_ref)], sems)
    lay_pieces(place, pieces, weight_ref)
    leaving = pltpu.make_async_copy(weight_ref, kept_ref, sems.at[1])
    leaving.start()
    wait_all(arriving)

    def run(at, part):
        conv = half_forward if at == 0 else half_spread
        value = base_ref[...] + conv(cols_ref, weight_ref, dims, part)
        if at == 0:
            value = value + take_clips(plan_ref, held_ref, dims)
        out_ref[...] = value.astype(jnp.bfloat16)

    on_half(section, 1 - near, run)
    leaving.wait()


def hand_out(place, ways, sums_ref, outs):
    if not ways:
        outs[0][...] = sums_ref[...]
        return
    rows = outs[0].shape[1]
    for at, out in enumerate(outs):
        for inner in (0, 1):
            owner = (place ^ (ways[at // 2] + at % 2 + 2 * inner)) % (sums_ref.shape[0] // rows)
            out[inner] = sums_ref[pl.ds(pl.multiple_of(owner * rows, ROW_TILE), rows), :]


def gradient_kernel(dims, split, plan_ref, clips_ref, cotangent_ref, gain_ref, last_gain_ref, mine_ref, theirs_ref,
                    early_cols_ref, grad_ref, hidden_ref, turned_ref, cols_ref, *rest):
    outs = rest[:-6]
    sums_ref, held_clips, held_cotangent, held_gain, held_last, sems = rest[-6:]
    section, place, near = where_am_i(split)
    channels = dims[4]
    total = dims[0] * dims[1] * dims[2] * dims[3]
    arriving = fetch(
        [
            (cotangent_ref, held_cotangent),
            (last_gain_ref, held_last),
            (clips_ref, held_clips),
            (gain_ref, held_gain),
        ],
        sems,
    )
    leading = section == 0
    mine = mine_ref[...].astype(jnp.float32)
    theirs = theirs_ref[...].astype(jnp.float32)
    hidden = jnp.where(leading, mine, theirs)
    spread = jnp.where(leading, theirs, mine)
    hidden_ref[...] = hidden.astype(jnp.bfloat16)
    wait_all(arriving)
    cotangent = held_cotangent[...].reshape(total, channels).astype(jnp.float32)
    upstream = back(hidden, cotangent, spread, held_last[...]).astype(jnp.bfloat16)
    grad_ref[...] = upstream
    unit = jnp.where(leading, take_clips(plan_ref, held_clips, dims), hidden)
    turned_ref[...] = activate(unit, held_gain[...]).T

    @pl.when(leading)
    def _():
        fill_columns(cols_ref, upstream.astype(jnp.float32), dims)

    @pl.when(jnp.logical_not(leading))
    def _():
        cols_ref[...] = early_cols_ref[...]

    for part in (0, 1):

        @pl.when(near != part)
        def _(part=part):
            half_gradient(turned_ref, cols_ref, sums_ref, dims, part)

    hand_out(place, (12, 8) if split else (), sums_ref, outs)


def rest_kernel(dims, split, turned_ref, cols_ref, *rest):
    outs, sums_ref = rest[:-1], rest[-1]
    section, place, near = where_am_i(split)
    for part in (0, 1):

        @pl.when(near == part)
        def _(part=part):
            half_gradient(turned_ref, cols_ref, sums_ref, dims, part)

    hand_out(place, (4, 0) if split else (), sums_ref, outs)


def last_kernel(dims, split, plan_ref, clips_ref, gain_ref, hidden_ref, grad_ref, near_ref, far_ref, acts_ref,
                grads_ref, weight_ref, cols_ref, held_clips, held_gain, held_hidden, held_grad, sems):
    section, place, near = where_am_i(split)
    half_rows = weight_ref.shape[0] // 2
    first = pl.multiple_of(near * half_rows, ROW_TILE) if split else 0
    second = pl.multiple_of((1 - near) * half_rows, ROW_TILE) if split else half_rows
    arriving = fetch(
        [
            (near_ref, weight_ref.at[pl.ds(first, half_rows)]),
            (far_ref, weight_ref.at[pl.ds(second, half_rows)]),
            (hidden_ref, held_hidden),
            (grad_ref, held_grad),
            (gain_ref, held_gain),
            (clips_ref, held_clips),
        ],
        sems,
    )
    wait_all(arriving)
    halves = weight_ref.at[pl.ds(0, half_rows)], weight_ref.at[pl.ds(half_rows, half_rows)]
    gain_row = held_gain[...]

    @pl.when(section == 0)
    def _():
        upstream = held_grad[...].astype(jnp.float32)
        fill_columns(cols_ref, upstream, dims)
        spread = half_spread(cols_ref, halves[0], dims, 0) + half_spread(cols_ref, halves[1], dims, 1)
        ordered = take_clips(plan_ref, held_clips, dims)
        grads_ref[...] = back(ordered, upstream, spread, gain_row).astype(jnp.bfloat16)
        acts_ref[...] = held_hidden[...]

    @pl.when(section != 0)
    def _():
        hidden = held_hidden[...].astype(jnp.float32)
        fill_columns(cols_ref, activate(hidden, gain_row).astype(jnp.float32), dims)
        branch = half_forward(cols_ref, halves[0], dims, 0) + half_forward(cols_ref, halves[1], dims, 1)
        acts_ref[...] = (hidden + branch).astype(jnp.bfloat16)
        grads_ref[...] = held_grad[...]


def swap(value, axis, by):
    return lax.ppermute(value, axis, [(i, i ^ by) for i in range(lax.axis_size(axis))])


def widen(value):
    return value.astype(jnp.float32)


def narrow(value):
    return value.astype(jnp.bfloat16)


def together(*values):
    return lax.optimization_barrier(values)


def on_device(clips, plan, gains, weights, cotangent):
    section = lax.axis_index("section")
    peers = lax.axis_size("fsdp")
    micro, frames, height, width, channels = clips.shape
    dims = clips.shape
    voxels = frames * height * width
    total = micro * voxels
    rows = weights.shape[1]
    all_rows = rows * peers
    half_rows = all_rows // 2
    factor = 1.0 / math.sqrt(peers * total)
    order = plan[0]
    flat_clips = clips.reshape(micro, voxels, channels)
    flat_cotangent = cotangent.reshape(micro, voxels, channels)
    split = peers == 16 and rows % ROW_TILE == 0

    smem = pl.BlockSpec(memory_space=pltpu.SMEM)
    vmem = pl.BlockSpec(memory_space=pltpu.VMEM)
    anywhere = pl.BlockSpec(memory_space=pl.ANY)
    half_weight = pltpu.VMEM((half_rows, channels), jnp.bfloat16)
    clips_scratch = pltpu.VMEM((micro, voxels, channels), jnp.bfloat16)
    volume_scratch = pltpu.VMEM((total, channels), jnp.bfloat16)
    gain_scratch = pltpu.VMEM((1, channels), jnp.float32)
    cols_shape = (micro, voxels + 2 * height * width, 9 * channels)
    volume = jax.ShapeDtypeStruct((total, channels), jnp.bfloat16)
    turned_out = jax.ShapeDtypeStruct((channels, total), jnp.bfloat16)
    cols_out = jax.ShapeDtypeStruct(cols_shape, jnp.bfloat16)
    half_out = jax.ShapeDtypeStruct((half_rows, channels), jnp.bfloat16)
    token_out = jax.ShapeDtypeStruct((8, 128), jnp.float32)

    def call(kernel, share, *, limit=VMEM_LIMIT, **config):
        flops = int(2 * total * all_rows * channels * share)
        return pl.pallas_call(
            functools.partial(kernel, dims, split),
            compiler_params=pltpu.CompilerParams(vmem_limit_bytes=limit),
            cost_estimate=pl.CostEstimate(flops=flops, bytes_accessed=2 * all_rows * channels, transcendentals=0),
            **config,
        )

    other_gain = swap(gains, "section", 1)
    last_gain = jnp.where(section == 0, other_gain, gains)

    early_cols, token = call(
        prepare_kernel,
        0.2,
        out_shape=[cols_out, token_out],
        in_specs=[smem] + [vmem] * 3 + [anywhere],
        out_specs=[vmem] * 2,
    )(order, flat_clips, flat_cotangent, gains, last_gain)

    own = weights[0]
    if split:
        held = {0: own}
        held[2] = swap(own, "fsdp", 2)
        held[4] = swap(own, "fsdp", 4)
        held[8] = swap(own, "fsdp", 8)
        held[4], held[2], token = together(held[4], held[2], token)
        held[6] = swap(held[4], "fsdp", 2)
        held[12] = swap(held[8], "fsdp", 4)
        held[8], held[6] = together(held[8], held[6])
        held[10] = swap(held[8], "fsdp", 2)
        held[14] = swap(held[12], "fsdp", 2)
        for by in (0, 2, 4, 6):
            held[by + 1] = swap(held[by], "fsdp", 1)
        near = [held[by] for by in range(8)]
    else:
        full = lax.all_gather(own, "fsdp", axis=0, tiled=True)
        near, far = [full[:half_rows]], [full[half_rows:]]
    count = len(near)

    base, token, near_weight = call(
        lambda dims, split, *refs: near_kernel(dims, split, count, *refs),
        0.5,
        out_shape=[jax.ShapeDtypeStruct((total, channels), jnp.float32), token_out, half_out],
        in_specs=[vmem] * (2 + count),
        out_specs=[vmem] * 2 + [anywhere],
        scratch_shapes=[half_weight, pltpu.SemaphoreType.DMA((1,))],
    )(early_cols, token, *near)

    if split:
        held[14], token = together(held[14], token)
        for by in (8, 10, 12, 14):
            held[by + 1] = swap(held[by], "fsdp", 1)
        far = [held[by] for by in range(8, 16)]

    mine, far_weight = call(
        lambda dims, split, *refs: far_kernel(dims, split, count, *refs),
        0.5,
        out_shape=[volume, half_out],
        in_specs=[smem] + [anywhere] * 2 + [vmem] * (2 + count),
        out_specs=[vmem, anywhere],
        scratch_shapes=[half_weight, clips_scratch, pltpu.SemaphoreType.DMA((2,))],
    )(order, flat_clips, token, early_cols, base, *far)

    theirs = swap(mine, "section", 1)

    shapes = [jax.ShapeDtypeStruct((2, rows, channels), jnp.bfloat16)] * 4 if split else [half_out]
    grad, hidden, turned, late_cols, *far_sums = call(
        gradient_kernel,
        0.5,
        out_shape=[volume, volume, turned_out, cols_out] + shapes,
        in_specs=[smem] + [anywhere] * 4 + [vmem] * 3,
        out_specs=[vmem] * (4 + len(shapes)),
        scratch_shapes=[
            half_weight,
            clips_scratch,
            clips_scratch,
            gain_scratch,
            gain_scratch,
            pltpu.SemaphoreType.DMA((4,)),
        ],
    )(order, flat_clips, flat_cotangent, gains, last_gain, mine, theirs, early_cols)

    near_sums = call(
        rest_kernel,
        0.5,
        out_shape=shapes,
        in_specs=[vmem] * 2,
        out_specs=[vmem] * len(shapes),
        scratch_shapes=[half_weight],
    )(turned, late_cols)

    if split:

        def core_sum(kept, sent):
            both = widen(kept) + widen(swap(sent, "fsdp", 1))
            return both[0], narrow(both[1])

        kept_12, send_12 = core_sum(*far_sums[:2])
        kept_8, send_8 = core_sum(*far_sums[2:])
        kept_4, send_4 = core_sum(*near_sums[:2])
        kept_0, send_0 = core_sum(*near_sums[2:])
        came_12 = swap(send_12, "fsdp", 2)
        came_12, send_8 = together(came_12, send_8)
        came_8 = swap(send_8, "fsdp", 2)
        from_4 = swap(narrow(kept_12 + widen(came_12)), "fsdp", 4)
        came_8, send_4 = together(came_8, send_4)
        came_4 = swap(send_4, "fsdp", 2)
        ready = narrow(kept_8 + widen(came_8) + widen(from_4))
        from_8 = swap(ready, "fsdp", 8)
        came_4, send_0 = together(came_4, send_0)
        came_0 = swap(send_0, "fsdp", 2)
        late = swap(narrow(kept_4 + widen(came_4)), "fsdp", 4)
        weight_grad = (kept_0 + widen(came_0) + widen(late) + widen(from_8)) * factor
        grad, _ = together(grad, ready)
    else:
        summed = widen(jnp.concatenate([near_sums[0], far_sums[0]], axis=0))
        weight_grad = lax.psum_scatter(summed, "fsdp", scatter_dimension=0, tiled=True) * factor

    acts, grads = call(
        last_kernel,
        1.0,
        limit=LAST_VMEM_LIMIT,
        out_shape=[volume, volume],
        in_specs=[smem] + [anywhere] * 6,
        out_specs=[vmem, vmem],
        scratch_shapes=[
            pltpu.VMEM((all_rows, channels), jnp.bfloat16),
            pltpu.VMEM(cols_shape, jnp.bfloat16),
            clips_scratch,
            gain_scratch,
            volume_scratch,
            volume_scratch,
            pltpu.SemaphoreType.DMA((6,)),
        ],
    )(order, flat_clips, gains, hidden, grad, near_weight, far_weight)
    return (acts.reshape(1, *dims), grads.reshape(1, *dims), weight_grad[None])


def solution(mesh):
    placed = (
        P("fsdp", None, None, None, None),
        P("fsdp", None),
        P("section", None),
        P("section", "fsdp", None),
        P("fsdp", None, None, None, None),
    )
    return jax.shard_map(
        on_device,
        mesh=mesh,
        in_specs=placed,
        out_specs=(
            P("section", "fsdp", None, None, None, None),
            P("section", "fsdp", None, None, None, None),
            P("section", "fsdp", None),
        ),
        check_vma=False,
    )
```

```python
import functools
import math

import jax
import jax.numpy as jnp
from jax import lax
from jax.experimental import pallas as pl
from jax.experimental.pallas import tpu as pltpu
from jax.sharding import PartitionSpec as P

EPSILON = 1e-06
ROW_TILE = 16
VMEM_LIMIT = 20 * 1024 * 1024
LAST_VMEM_LIMIT = 24 * 1024 * 1024


def normalize(values, gain_row):
    inverse = lax.rsqrt(jnp.mean(values * values, axis=-1, keepdims=True) + EPSILON)
    return inverse, values * inverse * gain_row


def activate(values, gain_row):
    inverse, normed = normalize(values, gain_row)
    return jnp.maximum(normed, 0.0).astype(jnp.bfloat16)


def back(values, upstream, spread, gain_row):
    inverse, normed = normalize(values, gain_row)
    scaled = gain_row * jnp.where(normed > 0.0, spread, 0.0)
    mixing = jnp.mean(values * scaled, axis=-1, keepdims=True)
    return upstream + inverse * scaled - values * (inverse * inverse * inverse) * mixing


def fill_columns(cols_ref, values, dims):
    micro, frames, height, width, channels = dims
    plane = height * width
    voxels = frames * plane
    total = micro * voxels
    row = lax.broadcasted_iota(jnp.int32, (plane, channels), 0)
    across = row % width
    down = row // width
    zero = jnp.zeros((micro, plane, cols_ref.shape[2]), jnp.bfloat16)
    cols_ref[:, :plane, :] = zero
    cols_ref[:, plane + voxels :, :] = zero

    def masked(rolled, inside):
        kept = rolled.reshape(total // plane, plane, channels) * inside.astype(jnp.float32)[None]
        return kept.reshape(total, channels)

    for by_w in (-1, 0, 1):
        if by_w == 0:
            along = values
        else:
            inside = (across + by_w >= 0) & (across + by_w < width)
            along = masked(pltpu.roll(values, (-by_w) % total, 0), inside)
        for by_h in (-1, 0, 1):
            if by_h == 0:
                moved = along
            else:
                inside = (down + by_h >= 0) & (down + by_h < height)
                moved = masked(pltpu.roll(along, (-by_h * width) % total, 0), inside)
            j = 3 * (by_h + 1) + by_w + 1
            cols_ref[:, plane : plane + voxels, j * channels : (j + 1) * channels] = moved.astype(
                jnp.bfloat16
            ).reshape(micro, voxels, channels)


def frame_columns(cols_ref, by_t, dims, begin, end):
    micro, frames, height, width, channels = dims
    plane = height * width
    voxels = frames * plane
    start = plane * (by_t + 1)
    return cols_ref[:, start : start + voxels, begin:end].reshape(micro * voxels, end - begin)


def half_pieces(half, dims):
    channels = dims[4]
    middle = channels // 2
    parts = []
    at = 0
    for k in range(14) if half == 0 else range(13, 27):
        low, high = 0, channels
        if k == 13:
            low, high = (0, middle) if half == 0 else (middle, channels)
        parts.append((k, low, high, at))
        at += high - low
    return parts


def half_forward(cols_ref, weight_ref, dims, half):
    channels = dims[4]
    middle = 9 * channels // 2
    if half == 0:
        runs = ((-1, 0, 2 * middle, 0), (0, 0, middle, 2 * middle))
    else:
        runs = ((0, middle, 2 * middle, 0), (1, 0, 2 * middle, middle))
    terms = [
        jnp.dot(
            frame_columns(cols_ref, by_t, dims, begin, end),
            weight_ref[at : at + end - begin, :],
            preferred_element_type=jnp.float32,
        )
        for by_t, begin, end, at in runs
    ]
    return terms[0] + terms[1]


def half_spread(cols_ref, weight_ref, dims, half):
    channels = dims[4]
    total, partial = None, None
    for k, low, high, at in half_pieces(half, dims):
        by_t, j = (26 - k) // 9 - 1, (26 - k) % 9
        term = lax.dot_general(
            frame_columns(cols_ref, by_t, dims, j * channels, (j + 1) * channels),
            weight_ref[at : at + high - low, :],
            (((1,), (1,)), ((), ())),
            preferred_element_type=jnp.float32,
        )
        if high - low < channels:
            partial = term
        else:
            total = term if total is None else total + term
    middle = channels // 2
    if half == 0:
        return jnp.concatenate([total[:, :middle] + partial, total[:, middle:]], axis=1)
    return jnp.concatenate([total[:, :middle], total[:, middle:] + partial], axis=1)


def half_gradient(turned_ref, cols_ref, sums_ref, dims, half):
    channels = dims[4]
    for k, low, high, at in half_pieces(half, dims):
        by_t, j = (26 - k) // 9 - 1, (26 - k) % 9
        sums_ref[at : at + high - low, :] = jnp.dot(
            turned_ref[low:high, :],
            frame_columns(cols_ref, by_t, dims, j * channels, (j + 1) * channels),
            preferred_element_type=jnp.float32,
        ).astype(jnp.bfloat16)


def where_am_i(split):
    place = lax.axis_index("fsdp")
    near = place // (lax.axis_size("fsdp") // 2) if split else 0
    return lax.axis_index("section"), place, near


def lay_pieces(place, pieces, weight_ref):
    if len(pieces) == 1:
        weight_ref[...] = pieces[0][...]
        return
    for by, piece in enumerate(pieces):
        rows = piece.shape[0]
        start = pl.multiple_of(((place ^ by) % len(pieces)) * rows, ROW_TILE)
        weight_ref[pl.ds(start, rows), :] = piece[...]


def take_clips(plan_ref, clips_ref, dims):
    picked = [clips_ref[plan_ref[m]] for m in range(dims[0])]
    return jnp.concatenate(picked, axis=0).astype(jnp.float32)


def on_half(section, half, run):
    for at in (0, 1):
        for part in (0, 1):

            @pl.when((section == at) & (half == part))
            def _(at=at, part=part):
                run(at, part)


def fetch(pairs, sems):
    copies = [pltpu.make_async_copy(source, target, sems.at[at]) for at, (source, target) in enumerate(pairs)]
    for copy in copies:
        copy.start()
    return copies


def wait_all(copies):
    for copy in copies:
        copy.wait()


def prepare_kernel(dims, split, plan_ref, clips_ref, cotangent_ref, gain_ref, early_ref, cols_ref, token_ref):
    section, place, near = where_am_i(split)
    total = dims[0] * dims[1] * dims[2] * dims[3]
    active = activate(take_clips(plan_ref, clips_ref, dims), gain_ref[...])
    upstream = cotangent_ref[...].reshape(total, dims[4]).astype(jnp.float32)
    fill_columns(cols_ref, jnp.where(section == 0, active.astype(jnp.float32), upstream), dims)
    token_ref[...] = jnp.zeros_like(token_ref)


def near_kernel(dims, split, count, cols_ref, early_ref, *rest):
    pieces, (out_ref, token_ref, kept_ref, weight_ref, sems) = rest[:count], rest[count:]
    section, place, near = where_am_i(split)
    lay_pieces(place, pieces, weight_ref)
    copies = fetch([(weight_ref, kept_ref)], sems)

    def run(at, part):
        conv = half_forward if at == 0 else half_spread
        out_ref[...] = conv(cols_ref, weight_ref, dims, part)

    on_half(section, near, run)
    token_ref[...] = early_ref[...]
    wait_all(copies)


def split_gain(gain_row):
    high = gain_row.astype(jnp.bfloat16).astype(jnp.float32)
    middle = (gain_row - high).astype(jnp.bfloat16).astype(jnp.float32)
    low = gain_row - high - middle
    row = lax.broadcasted_iota(jnp.int32, (ROW_TILE, gain_row.shape[1]), 0)
    parts = jnp.where(row == 0, high, jnp.where(row == 1, middle, jnp.where(row == 2, low, 0.0)))
    return parts.astype(jnp.bfloat16)


def join_gain(parts):
    parts = parts.astype(jnp.float32)
    return (parts[0:1] + parts[1:2]) + parts[2:3]


def far_kernel(dims, split, count, plan_ref, clips_ref, gain_ref, early_ref, cols_ref, base_ref, *rest):
    pieces, (out_ref, kept_ref, weight_ref, held_ref, held_gain, sems) = rest[:count], rest[count:]
    total = base_ref.shape[0]
    section, place, near = where_am_i(split)
    arriving = fetch([(clips_ref, held_ref), (gain_ref, held_gain)], sems)
    lay_pieces(place, pieces, weight_ref)
    leaving = pltpu.make_async_copy(weight_ref, kept_ref, sems.at[2])
    leaving.start()
    wait_all(arriving)
    out_ref[total:, :] = split_gain(held_gain[...])

    def run(at, part):
        conv = half_forward if at == 0 else half_spread
        value = base_ref[...] + conv(cols_ref, weight_ref, dims, part)
        if at == 0:
            value = value + take_clips(plan_ref, held_ref, dims)
        out_ref[:total, :] = value.astype(jnp.bfloat16)

    on_half(section, 1 - near, run)
    leaving.wait()


def hand_out(place, ways, sums_ref, outs):
    if not ways:
        outs[0][...] = sums_ref[...]
        return
    rows = outs[0].shape[1]
    for at, out in enumerate(outs):
        for inner in (0, 1):
            owner = (place ^ (ways[at // 2] + at % 2 + 2 * inner)) % (sums_ref.shape[0] // rows)
            out[inner] = sums_ref[pl.ds(pl.multiple_of(owner * rows, ROW_TILE), rows), :]


def gradient_kernel(dims, split, plan_ref, clips_ref, cotangent_ref, gain_ref, mine_ref, theirs_ref,
                    early_cols_ref, grad_ref, hidden_ref, turned_ref, cols_ref, *rest):
    outs = rest[:-5]
    sums_ref, held_clips, held_cotangent, held_gain, sems = rest[-5:]
    section, place, near = where_am_i(split)
    channels = dims[4]
    total = dims[0] * dims[1] * dims[2] * dims[3]
    arriving = fetch(
        [
            (cotangent_ref, held_cotangent),
            (clips_ref, held_clips),
            (gain_ref, held_gain),
        ],
        sems,
    )
    leading = section == 0
    mine = mine_ref[:total, :].astype(jnp.float32)
    theirs = theirs_ref[:total, :].astype(jnp.float32)
    last_gain = join_gain(jnp.where(leading, theirs_ref[total:, :].astype(jnp.float32), mine_ref[total:, :].astype(jnp.float32)))
    hidden = jnp.where(leading, mine, theirs)
    spread = jnp.where(leading, theirs, mine)
    hidden_ref[...] = hidden.astype(jnp.bfloat16)
    wait_all(arriving)
    cotangent = held_cotangent[...].reshape(total, channels).astype(jnp.float32)
    upstream = back(hidden, cotangent, spread, last_gain).astype(jnp.bfloat16)
    grad_ref[...] = upstream
    unit = jnp.where(leading, take_clips(plan_ref, held_clips, dims), hidden)
    turned_ref[...] = activate(unit, held_gain[...]).T

    @pl.when(leading)
    def _():
        fill_columns(cols_ref, upstream.astype(jnp.float32), dims)

    @pl.when(jnp.logical_not(leading))
    def _():
        cols_ref[...] = early_cols_ref[...]

    for part in (0, 1):

        @pl.when(near != part)
        def _(part=part):
            half_gradient(turned_ref, cols_ref, sums_ref, dims, part)

    hand_out(place, (12, 8) if split else (), sums_ref, outs)


def rest_kernel(dims, split, turned_ref, cols_ref, *rest):
    outs, sums_ref = rest[:-1], rest[-1]
    section, place, near = where_am_i(split)
    for part in (0, 1):

        @pl.when(near == part)
        def _(part=part):
            half_gradient(turned_ref, cols_ref, sums_ref, dims, part)

    hand_out(place, (4, 0) if split else (), sums_ref, outs)


def last_kernel(dims, split, plan_ref, clips_ref, gain_ref, hidden_ref, grad_ref, near_ref, far_ref, acts_ref,
                grads_ref, weight_ref, cols_ref, held_clips, held_gain, held_hidden, held_grad, made_acts, made_grads, sems):
    section, place, near = where_am_i(split)
    half_rows = weight_ref.shape[0] // 2
    first = pl.multiple_of(near * half_rows, ROW_TILE) if split else 0
    second = pl.multiple_of((1 - near) * half_rows, ROW_TILE) if split else half_rows
    arriving = fetch(
        [
            (near_ref, weight_ref.at[pl.ds(first, half_rows)]),
            (far_ref, weight_ref.at[pl.ds(second, half_rows)]),
            (hidden_ref, held_hidden),
            (grad_ref, held_grad),
            (gain_ref, held_gain),
            (clips_ref, held_clips),
        ],
        sems,
    )
    wait_all(arriving)
    halves = weight_ref.at[pl.ds(0, half_rows)], weight_ref.at[pl.ds(half_rows, half_rows)]
    gain_row = held_gain[...]

    @pl.when(section == 0)
    def _():
        upstream = held_grad[...].astype(jnp.float32)
        fill_columns(cols_ref, upstream, dims)
        spread = half_spread(cols_ref, halves[0], dims, 0) + half_spread(cols_ref, halves[1], dims, 1)
        ordered = take_clips(plan_ref, held_clips, dims)
        back_out = back(ordered, upstream, spread, gain_row).astype(jnp.bfloat16)
        made_grads[...] = back_out.reshape(made_grads.shape)
        made_acts[...] = held_hidden[...].reshape(made_acts.shape)

    @pl.when(section != 0)
    def _():
        hidden = held_hidden[...].astype(jnp.float32)
        fill_columns(cols_ref, activate(hidden, gain_row).astype(jnp.float32), dims)
        branch = half_forward(cols_ref, halves[0], dims, 0) + half_forward(cols_ref, halves[1], dims, 1)
        made_acts[...] = (hidden + branch).astype(jnp.bfloat16).reshape(made_acts.shape)
        made_grads[...] = held_grad[...].reshape(made_grads.shape)

    wait_all(fetch([(made_acts, acts_ref), (made_grads, grads_ref)], sems))


def swap(value, axis, by):
    return lax.ppermute(value, axis, [(i, i ^ by) for i in range(lax.axis_size(axis))])


def widen(value):
    return value.astype(jnp.float32)


def narrow(value):
    return value.astype(jnp.bfloat16)


def together(*values):
    return lax.optimization_barrier(values)


def on_device(clips, plan, gains, weights, cotangent):
    peers = lax.axis_size("fsdp")
    micro, frames, height, width, channels = clips.shape
    dims = clips.shape
    voxels = frames * height * width
    total = micro * voxels
    rows = weights.shape[1]
    all_rows = rows * peers
    half_rows = all_rows // 2
    factor = 1.0 / math.sqrt(peers * total)
    order = plan[0]
    flat_clips = clips.reshape(micro, voxels, channels)
    flat_cotangent = cotangent.reshape(micro, voxels, channels)
    split = peers == 16 and rows % ROW_TILE == 0

    smem = pl.BlockSpec(memory_space=pltpu.SMEM)
    vmem = pl.BlockSpec(memory_space=pltpu.VMEM)
    anywhere = pl.BlockSpec(memory_space=pl.ANY)
    half_weight = pltpu.VMEM((half_rows, channels), jnp.bfloat16)
    clips_scratch = pltpu.VMEM((micro, voxels, channels), jnp.bfloat16)
    volume_scratch = pltpu.VMEM((total, channels), jnp.bfloat16)
    gain_scratch = pltpu.VMEM((1, channels), jnp.float32)
    cols_shape = (micro, voxels + 2 * height * width, 9 * channels)
    volume = jax.ShapeDtypeStruct((total, channels), jnp.bfloat16)
    turned_out = jax.ShapeDtypeStruct((channels, total), jnp.bfloat16)
    cols_out = jax.ShapeDtypeStruct(cols_shape, jnp.bfloat16)
    half_out = jax.ShapeDtypeStruct((half_rows, channels), jnp.bfloat16)
    token_out = jax.ShapeDtypeStruct((8, 128), jnp.float32)

    def call(kernel, share, *, limit=VMEM_LIMIT, **config):
        flops = int(2 * total * all_rows * channels * share)
        return pl.pallas_call(
            functools.partial(kernel, dims, split),
            compiler_params=pltpu.CompilerParams(vmem_limit_bytes=limit),
            cost_estimate=pl.CostEstimate(flops=flops, bytes_accessed=2 * all_rows * channels, transcendentals=0),
            **config,
        )

    own = weights[0]
    signal = gains
    if split:
        held = {0: own}
        held[2] = swap(own, "fsdp", 2)
        held[4] = swap(own, "fsdp", 4)
        held[8] = swap(own, "fsdp", 8)
        signal = held[4]

    early_cols, token = call(
        prepare_kernel,
        0.2,
        out_shape=[cols_out, token_out],
        in_specs=[smem] + [vmem] * 3 + [anywhere],
        out_specs=[vmem] * 2,
    )(order, flat_clips, flat_cotangent, gains, gains)

    if split:
        held[4], token = together(held[4], token)
        held[6] = swap(held[4], "fsdp", 2)
        held[12] = swap(held[8], "fsdp", 4)
        held[10] = swap(held[8], "fsdp", 2)
        held[14] = swap(held[12], "fsdp", 2)
        for by in (0, 2, 4, 6):
            held[by + 1] = swap(held[by], "fsdp", 1)
        near = [held[by] for by in range(8)]
    else:
        full = lax.all_gather(own, "fsdp", axis=0, tiled=True)
        near, far = [full[:half_rows]], [full[half_rows:]]
    count = len(near)

    base, token, near_weight = call(
        lambda dims, split, *refs: near_kernel(dims, split, count, *refs),
        0.5,
        out_shape=[jax.ShapeDtypeStruct((total, channels), jnp.float32), token_out, half_out],
        in_specs=[vmem] * (2 + count),
        out_specs=[vmem] * 2 + [anywhere],
        scratch_shapes=[half_weight, pltpu.SemaphoreType.DMA((1,))],
    )(early_cols, token, *near)

    if split:
        held[14], token = together(held[14], token)
        for by in (8, 10, 12, 14):
            held[by + 1] = swap(held[by], "fsdp", 1)
        far = [held[by] for by in range(8, 16)]

    mine, far_weight = call(
        lambda dims, split, *refs: far_kernel(dims, split, count, *refs),
        0.5,
        out_shape=[jax.ShapeDtypeStruct((total + ROW_TILE, channels), jnp.bfloat16), half_out],
        in_specs=[smem] + [anywhere] * 3 + [vmem] * (2 + count),
        out_specs=[vmem, anywhere],
        scratch_shapes=[half_weight, clips_scratch, gain_scratch, pltpu.SemaphoreType.DMA((3,))],
    )(order, flat_clips, gains, token, early_cols, base, *far)

    theirs = swap(mine, "section", 1)

    shapes = [jax.ShapeDtypeStruct((2, rows, channels), jnp.bfloat16)] * 4 if split else [half_out]
    grad, hidden, turned, late_cols, *far_sums = call(
        gradient_kernel,
        0.5,
        out_shape=[volume, volume, turned_out, cols_out] + shapes,
        in_specs=[smem] + [anywhere] * 3 + [vmem] * 3,
        out_specs=[vmem] * (4 + len(shapes)),
        scratch_shapes=[
            half_weight,
            clips_scratch,
            clips_scratch,
            gain_scratch,
            pltpu.SemaphoreType.DMA((3,)),
        ],
    )(order, flat_clips, flat_cotangent, gains, mine, theirs, early_cols)

    near_sums = call(
        rest_kernel,
        0.5,
        out_shape=shapes,
        in_specs=[vmem] * 2,
        out_specs=[vmem] * len(shapes),
        scratch_shapes=[half_weight],
    )(turned, late_cols)

    if split:

        def core_sum(kept, sent):
            both = widen(kept) + widen(swap(sent, "fsdp", 1))
            return both[0], narrow(both[1])

        kept_12, send_12 = core_sum(*far_sums[:2])
        kept_8, send_8 = core_sum(*far_sums[2:])
        kept_4, send_4 = core_sum(*near_sums[:2])
        kept_0, send_0 = core_sum(*near_sums[2:])
        came_12 = swap(send_12, "fsdp", 2)
        came_12, send_8 = together(came_12, send_8)
        came_8 = swap(send_8, "fsdp", 2)
        from_4 = swap(narrow(kept_12 + widen(came_12)), "fsdp", 4)
        came_8, send_4 = together(came_8, send_4)
        came_4 = swap(send_4, "fsdp", 2)
        ready = narrow(kept_8 + widen(came_8) + widen(from_4))
        from_8 = swap(ready, "fsdp", 8)
        came_4, send_0 = together(came_4, send_0)
        came_0 = swap(send_0, "fsdp", 2)
        late = swap(narrow(kept_4 + widen(came_4)), "fsdp", 4)
        weight_grad = (kept_0 + widen(came_0) + widen(late) + widen(from_8)) * factor
        grad, _ = together(grad, ready)
    else:
        summed = widen(jnp.concatenate([near_sums[0], far_sums[0]], axis=0))
        weight_grad = lax.psum_scatter(summed, "fsdp", scatter_dimension=0, tiled=True) * factor

    acts, grads = call(
        last_kernel,
        1.0,
        limit=LAST_VMEM_LIMIT,
        out_shape=[jax.ShapeDtypeStruct((1, *dims), jnp.bfloat16)] * 2,
        in_specs=[smem] + [anywhere] * 6,
        out_specs=[anywhere, anywhere],
        scratch_shapes=[
            pltpu.VMEM((all_rows, channels), jnp.bfloat16),
            pltpu.VMEM(cols_shape, jnp.bfloat16),
            clips_scratch,
            gain_scratch,
            volume_scratch,
            volume_scratch,
            pltpu.VMEM((1, *dims), jnp.bfloat16),
            pltpu.VMEM((1, *dims), jnp.bfloat16),
            pltpu.SemaphoreType.DMA((6,)),
        ],
    )(order, flat_clips, gains, hidden, grad, near_weight, far_weight)
    return (acts, grads, weight_grad[None])


def solution(mesh):
    placed = (
        P("fsdp", None, None, None, None),
        P("fsdp", None),
        P("section", None),
        P("section", "fsdp", None),
        P("fsdp", None, None, None, None),
    )
    return jax.shard_map(
        on_device,
        mesh=mesh,
        in_specs=placed,
        out_specs=(
            P("section", "fsdp", None, None, None, None),
            P("section", "fsdp", None, None, None, None),
            P("section", "fsdp", None),
        ),
        check_vma=False,
    )
```

```python
import functools
import math

import jax
import jax.numpy as jnp
from jax import lax
from jax.experimental import pallas as pl
from jax.experimental.pallas import tpu as pltpu
from jax.sharding import PartitionSpec as P

EPSILON = 1e-06
ROW_TILE = 16
VMEM_LIMIT = 20 * 1024 * 1024
LAST_VMEM_LIMIT = 24 * 1024 * 1024


def normalize(values, gain_row):
    inverse = lax.rsqrt(jnp.mean(values * values, axis=-1, keepdims=True) + EPSILON)
    return inverse, values * inverse * gain_row


def activate(values, gain_row):
    inverse, normed = normalize(values, gain_row)
    return jnp.maximum(normed, 0.0).astype(jnp.bfloat16)


def back(values, upstream, spread, gain_row):
    inverse, normed = normalize(values, gain_row)
    scaled = gain_row * jnp.where(normed > 0.0, spread, 0.0)
    mixing = jnp.mean(values * scaled, axis=-1, keepdims=True)
    return upstream + inverse * scaled - values * (inverse * inverse * inverse) * mixing


def fill_columns(cols_ref, values, dims):
    micro, frames, height, width, channels = dims
    plane = height * width
    voxels = frames * plane
    total = micro * voxels
    row = lax.broadcasted_iota(jnp.int32, (plane, channels), 0)
    across = row % width
    down = row // width
    zero = jnp.zeros((micro, plane, cols_ref.shape[2]), jnp.bfloat16)
    cols_ref[:, :plane, :] = zero
    cols_ref[:, plane + voxels :, :] = zero

    def masked(rolled, inside):
        kept = rolled.reshape(total // plane, plane, channels) * inside.astype(jnp.float32)[None]
        return kept.reshape(total, channels)

    for by_w in (-1, 0, 1):
        if by_w == 0:
            along = values
        else:
            inside = (across + by_w >= 0) & (across + by_w < width)
            along = masked(pltpu.roll(values, (-by_w) % total, 0), inside)
        for by_h in (-1, 0, 1):
            if by_h == 0:
                moved = along
            else:
                inside = (down + by_h >= 0) & (down + by_h < height)
                moved = masked(pltpu.roll(along, (-by_h * width) % total, 0), inside)
            j = 3 * (by_h + 1) + by_w + 1
            cols_ref[:, plane : plane + voxels, j * channels : (j + 1) * channels] = moved.astype(
                jnp.bfloat16
            ).reshape(micro, voxels, channels)


def frame_columns(cols_ref, by_t, dims, begin, end):
    micro, frames, height, width, channels = dims
    plane = height * width
    voxels = frames * plane
    start = plane * (by_t + 1)
    return cols_ref[:, start : start + voxels, begin:end].reshape(micro * voxels, end - begin)


def half_pieces(half, dims):
    channels = dims[4]
    middle = channels // 2
    parts = []
    at = 0
    for k in range(14) if half == 0 else range(13, 27):
        low, high = 0, channels
        if k == 13:
            low, high = (0, middle) if half == 0 else (middle, channels)
        parts.append((k, low, high, at))
        at += high - low
    return parts


def half_forward(cols_ref, weight_ref, dims, half):
    channels = dims[4]
    middle = 9 * channels // 2
    if half == 0:
        runs = ((-1, 0, 2 * middle, 0), (0, 0, middle, 2 * middle))
    else:
        runs = ((0, middle, 2 * middle, 0), (1, 0, 2 * middle, middle))
    terms = [
        jnp.dot(
            frame_columns(cols_ref, by_t, dims, begin, end),
            weight_ref[at : at + end - begin, :],
            preferred_element_type=jnp.float32,
        )
        for by_t, begin, end, at in runs
    ]
    return terms[0] + terms[1]


def half_spread(cols_ref, weight_ref, dims, half):
    channels = dims[4]
    total, partial = None, None
    for k, low, high, at in half_pieces(half, dims):
        by_t, j = (26 - k) // 9 - 1, (26 - k) % 9
        term = lax.dot_general(
            frame_columns(cols_ref, by_t, dims, j * channels, (j + 1) * channels),
            weight_ref[at : at + high - low, :],
            (((1,), (1,)), ((), ())),
            preferred_element_type=jnp.float32,
        )
        if high - low < channels:
            partial = term
        else:
            total = term if total is None else total + term
    middle = channels // 2
    if half == 0:
        return jnp.concatenate([total[:, :middle] + partial, total[:, middle:]], axis=1)
    return jnp.concatenate([total[:, :middle], total[:, middle:] + partial], axis=1)


def half_gradient(turned_ref, cols_ref, sums_ref, dims, half):
    channels = dims[4]
    for k, low, high, at in half_pieces(half, dims):
        by_t, j = (26 - k) // 9 - 1, (26 - k) % 9
        sums_ref[at : at + high - low, :] = jnp.dot(
            turned_ref[low:high, :],
            frame_columns(cols_ref, by_t, dims, j * channels, (j + 1) * channels),
            preferred_element_type=jnp.float32,
        ).astype(jnp.bfloat16)


def where_am_i(split):
    place = lax.axis_index("fsdp")
    near = place // (lax.axis_size("fsdp") // 2) if split else 0
    return lax.axis_index("section"), place, near


def lay_pieces(place, pieces, weight_ref):
    if len(pieces) == 1:
        weight_ref[...] = pieces[0][...]
        return
    for by, piece in enumerate(pieces):
        rows = piece.shape[0]
        start = pl.multiple_of(((place ^ by) % len(pieces)) * rows, ROW_TILE)
        weight_ref[pl.ds(start, rows), :] = piece[...]


def take_clips(plan_ref, clips_ref, dims):
    picked = [clips_ref[plan_ref[m]] for m in range(dims[0])]
    return jnp.concatenate(picked, axis=0).astype(jnp.float32)


def on_half(section, half, run):
    for at in (0, 1):
        for part in (0, 1):

            @pl.when((section == at) & (half == part))
            def _(at=at, part=part):
                run(at, part)


def fetch(pairs, sems):
    copies = [pltpu.make_async_copy(source, target, sems.at[at]) for at, (source, target) in enumerate(pairs)]
    for copy in copies:
        copy.start()
    return copies


def wait_all(copies):
    for copy in copies:
        copy.wait()


def prepare_kernel(dims, split, plan_ref, clips_ref, cotangent_ref, gain_ref, early_ref, cols_ref, token_ref):
    section, place, near = where_am_i(split)
    total = dims[0] * dims[1] * dims[2] * dims[3]
    active = activate(take_clips(plan_ref, clips_ref, dims), gain_ref[...])
    upstream = cotangent_ref[...].reshape(total, dims[4]).astype(jnp.float32)
    fill_columns(cols_ref, jnp.where(section == 0, active.astype(jnp.float32), upstream), dims)
    token_ref[...] = jnp.zeros_like(token_ref)


def near_kernel(dims, split, count, cols_ref, early_ref, *rest):
    pieces, (out_ref, token_ref, kept_ref, weight_ref, sems) = rest[:count], rest[count:]
    section, place, near = where_am_i(split)
    lay_pieces(place, pieces, weight_ref)
    copies = fetch([(weight_ref, kept_ref)], sems)

    def run(at, part):
        conv = half_forward if at == 0 else half_spread
        out_ref[...] = conv(cols_ref, weight_ref, dims, part)

    on_half(section, near, run)
    token_ref[...] = early_ref[...]
    wait_all(copies)


def split_gain(gain_row):
    high = gain_row.astype(jnp.bfloat16).astype(jnp.float32)
    middle = (gain_row - high).astype(jnp.bfloat16).astype(jnp.float32)
    low = gain_row - high - middle
    row = lax.broadcasted_iota(jnp.int32, (ROW_TILE, gain_row.shape[1]), 0)
    parts = jnp.where(row == 0, high, jnp.where(row == 1, middle, jnp.where(row == 2, low, 0.0)))
    return parts.astype(jnp.bfloat16)


def join_gain(parts):
    parts = parts.astype(jnp.float32)
    return (parts[0:1] + parts[1:2]) + parts[2:3]


def far_kernel(dims, split, count, plan_ref, clips_ref, gain_ref, early_ref, cols_ref, base_ref, *rest):
    pieces, (out_ref, kept_ref, weight_ref, held_ref, held_gain, sems) = rest[:count], rest[count:]
    total = base_ref.shape[0]
    section, place, near = where_am_i(split)
    arriving = fetch([(clips_ref, held_ref), (gain_ref, held_gain)], sems)
    lay_pieces(place, pieces, weight_ref)
    leaving = pltpu.make_async_copy(weight_ref, kept_ref, sems.at[2])
    leaving.start()
    wait_all(arriving)
    out_ref[total:, :] = split_gain(held_gain[...])

    def run(at, part):
        conv = half_forward if at == 0 else half_spread
        value = base_ref[...] + conv(cols_ref, weight_ref, dims, part)
        if at == 0:
            value = value + take_clips(plan_ref, held_ref, dims)
        out_ref[:total, :] = value.astype(jnp.bfloat16)

    on_half(section, 1 - near, run)
    leaving.wait()


def hand_out(place, ways, sums_ref, outs):
    if not ways:
        outs[0][...] = sums_ref[...]
        return
    rows = outs[0].shape[1]
    for at, out in enumerate(outs):
        for inner in (0, 1):
            owner = (place ^ (ways[at // 2] + at % 2 + 2 * inner)) % (sums_ref.shape[0] // rows)
            out[inner] = sums_ref[pl.ds(pl.multiple_of(owner * rows, ROW_TILE), rows), :]


def gradient_kernel(dims, split, plan_ref, clips_ref, cotangent_ref, gain_ref, mine_ref, theirs_ref,
                    early_cols_ref, grad_ref, hidden_ref, turned_ref, cols_ref, *rest):
    outs = rest[:-5]
    sums_ref, held_clips, held_cotangent, held_gain, sems = rest[-5:]
    section, place, near = where_am_i(split)
    channels = dims[4]
    total = dims[0] * dims[1] * dims[2] * dims[3]
    arriving = fetch(
        [
            (cotangent_ref, held_cotangent),
            (clips_ref, held_clips),
            (gain_ref, held_gain),
        ],
        sems,
    )
    leading = section == 0
    mine = mine_ref[:total, :].astype(jnp.float32)
    theirs = theirs_ref[:total, :].astype(jnp.float32)
    last_gain = join_gain(jnp.where(leading, theirs_ref[total:, :].astype(jnp.float32), mine_ref[total:, :].astype(jnp.float32)))
    hidden = jnp.where(leading, mine, theirs)
    spread = jnp.where(leading, theirs, mine)
    hidden_ref[...] = hidden.astype(jnp.bfloat16)
    wait_all(arriving)
    cotangent = held_cotangent[...].reshape(total, channels).astype(jnp.float32)
    upstream = back(hidden, cotangent, spread, last_gain).astype(jnp.bfloat16)
    grad_ref[...] = upstream
    unit = jnp.where(leading, take_clips(plan_ref, held_clips, dims), hidden)
    turned_ref[...] = activate(unit, held_gain[...]).T

    @pl.when(leading)
    def _():
        fill_columns(cols_ref, upstream.astype(jnp.float32), dims)

    @pl.when(jnp.logical_not(leading))
    def _():
        cols_ref[...] = early_cols_ref[...]

    for part in (0, 1):

        @pl.when(near != part)
        def _(part=part):
            half_gradient(turned_ref, cols_ref, sums_ref, dims, part)

    hand_out(place, (12, 8) if split else (), sums_ref, outs)


def rest_kernel(dims, split, turned_ref, cols_ref, *rest):
    outs, sums_ref = rest[:-1], rest[-1]
    section, place, near = where_am_i(split)
    for part in (0, 1):

        @pl.when(near == part)
        def _(part=part):
            half_gradient(turned_ref, cols_ref, sums_ref, dims, part)

    hand_out(place, (4, 0) if split else (), sums_ref, outs)


def last_kernel(dims, split, plan_ref, clips_ref, gain_ref, hidden_ref, grad_ref, near_ref, far_ref, acts_ref,
                grads_ref, weight_ref, cols_ref, held_clips, held_gain, held_hidden, held_grad, made_acts, made_grads, sems):
    section, place, near = where_am_i(split)
    half_rows = weight_ref.shape[0] // 2
    first = pl.multiple_of(near * half_rows, ROW_TILE) if split else 0
    second = pl.multiple_of((1 - near) * half_rows, ROW_TILE) if split else half_rows
    arriving = fetch(
        [
            (near_ref, weight_ref.at[pl.ds(first, half_rows)]),
            (far_ref, weight_ref.at[pl.ds(second, half_rows)]),
            (hidden_ref, held_hidden),
            (grad_ref, held_grad),
            (gain_ref, held_gain),
            (clips_ref, held_clips),
        ],
        sems,
    )
    wait_all(arriving)
    halves = weight_ref.at[pl.ds(0, half_rows)], weight_ref.at[pl.ds(half_rows, half_rows)]
    gain_row = held_gain[...]

    @pl.when(section == 0)
    def _():
        upstream = held_grad[...].astype(jnp.float32)
        fill_columns(cols_ref, upstream, dims)
        spread = half_spread(cols_ref, halves[0], dims, 0) + half_spread(cols_ref, halves[1], dims, 1)
        ordered = take_clips(plan_ref, held_clips, dims)
        back_out = back(ordered, upstream, spread, gain_row).astype(jnp.bfloat16)
        made_grads[...] = back_out.reshape(made_grads.shape)
        made_acts[...] = held_hidden[...].reshape(made_acts.shape)

    @pl.when(section != 0)
    def _():
        hidden = held_hidden[...].astype(jnp.float32)
        fill_columns(cols_ref, activate(hidden, gain_row).astype(jnp.float32), dims)
        branch = half_forward(cols_ref, halves[0], dims, 0) + half_forward(cols_ref, halves[1], dims, 1)
        made_acts[...] = (hidden + branch).astype(jnp.bfloat16).reshape(made_acts.shape)
        made_grads[...] = held_grad[...].reshape(made_grads.shape)

    wait_all(fetch([(made_acts, acts_ref), (made_grads, grads_ref)], sems))


def swap(value, axis, by):
    return lax.ppermute(value, axis, [(i, i ^ by) for i in range(lax.axis_size(axis))])


def widen(value):
    return value.astype(jnp.float32)


def narrow(value):
    return value.astype(jnp.bfloat16)


def together(*values):
    return lax.optimization_barrier(values)


def on_device(clips, plan, gains, weights, cotangent):
    peers = lax.axis_size("fsdp")
    micro, frames, height, width, channels = clips.shape
    dims = clips.shape
    voxels = frames * height * width
    total = micro * voxels
    rows = weights.shape[1]
    all_rows = rows * peers
    half_rows = all_rows // 2
    factor = 1.0 / math.sqrt(peers * total)
    order = plan[0]
    flat_clips = clips.reshape(micro, voxels, channels)
    flat_cotangent = cotangent.reshape(micro, voxels, channels)
    split = peers == 16 and rows % ROW_TILE == 0

    smem = pl.BlockSpec(memory_space=pltpu.SMEM)
    vmem = pl.BlockSpec(memory_space=pltpu.VMEM)
    anywhere = pl.BlockSpec(memory_space=pl.ANY)
    half_weight = pltpu.VMEM((half_rows, channels), jnp.bfloat16)
    clips_scratch = pltpu.VMEM((micro, voxels, channels), jnp.bfloat16)
    volume_scratch = pltpu.VMEM((total, channels), jnp.bfloat16)
    gain_scratch = pltpu.VMEM((1, channels), jnp.float32)
    cols_shape = (micro, voxels + 2 * height * width, 9 * channels)
    volume = jax.ShapeDtypeStruct((total, channels), jnp.bfloat16)
    turned_out = jax.ShapeDtypeStruct((channels, total), jnp.bfloat16)
    cols_out = jax.ShapeDtypeStruct(cols_shape, jnp.bfloat16)
    half_out = jax.ShapeDtypeStruct((half_rows, channels), jnp.bfloat16)
    token_out = jax.ShapeDtypeStruct((8, 128), jnp.float32)

    def call(kernel, share, *, limit=VMEM_LIMIT, **config):
        flops = int(2 * total * all_rows * channels * share)
        return pl.pallas_call(
            functools.partial(kernel, dims, split),
            compiler_params=pltpu.CompilerParams(vmem_limit_bytes=limit),
            cost_estimate=pl.CostEstimate(flops=flops, bytes_accessed=2 * all_rows * channels, transcendentals=0),
            **config,
        )

    own = weights[0]
    signal = gains
    if split:
        held = {0: own}
        held[2] = swap(own, "fsdp", 2)
        held[4] = swap(own, "fsdp", 4)
        held[8] = swap(own, "fsdp", 8)
        signal = held[4]

    early_cols, token = call(
        prepare_kernel,
        0.2,
        out_shape=[cols_out, token_out],
        in_specs=[smem] + [vmem] * 3 + [anywhere],
        out_specs=[vmem] * 2,
    )(order, flat_clips, flat_cotangent, gains, gains)

    if split:
        held[4], token = together(held[4], token)
        held[6] = swap(held[4], "fsdp", 2)
        held[12] = swap(held[8], "fsdp", 4)
        held[10] = swap(held[8], "fsdp", 2)
        held[14] = swap(held[12], "fsdp", 2)
        for by in (0, 2, 4, 6):
            held[by + 1] = swap(held[by], "fsdp", 1)
        near = [held[by] for by in range(8)]
    else:
        full = lax.all_gather(own, "fsdp", axis=0, tiled=True)
        near, far = [full[:half_rows]], [full[half_rows:]]
    count = len(near)

    base, token, near_weight = call(
        lambda dims, split, *refs: near_kernel(dims, split, count, *refs),
        0.5,
        out_shape=[jax.ShapeDtypeStruct((total, channels), jnp.float32), token_out, half_out],
        in_specs=[vmem] * (2 + count),
        out_specs=[vmem] * 2 + [anywhere],
        scratch_shapes=[half_weight, pltpu.SemaphoreType.DMA((1,))],
    )(early_cols, token, *near)

    if split:
        held[14], token = together(held[14], token)
        for by in (8, 10, 12, 14):
            held[by + 1] = swap(held[by], "fsdp", 1)
        far = [held[by] for by in range(8, 16)]

    mine, far_weight = call(
        lambda dims, split, *refs: far_kernel(dims, split, count, *refs),
        0.5,
        out_shape=[jax.ShapeDtypeStruct((total + ROW_TILE, channels), jnp.bfloat16), half_out],
        in_specs=[smem] + [anywhere] * 3 + [vmem] * (2 + count),
        out_specs=[vmem, anywhere],
        scratch_shapes=[half_weight, clips_scratch, gain_scratch, pltpu.SemaphoreType.DMA((3,))],
    )(order, flat_clips, gains, token, early_cols, base, *far)

    theirs = swap(mine, "section", 1)

    shapes = [jax.ShapeDtypeStruct((2, rows, channels), jnp.bfloat16)] * 4 if split else [half_out]
    grad, hidden, turned, late_cols, *far_sums = call(
        gradient_kernel,
        0.5,
        out_shape=[volume, volume, turned_out, cols_out] + shapes,
        in_specs=[smem] + [anywhere] * 3 + [vmem] * 3,
        out_specs=[vmem] * (4 + len(shapes)),
        scratch_shapes=[
            half_weight,
            clips_scratch,
            clips_scratch,
            gain_scratch,
            pltpu.SemaphoreType.DMA((3,)),
        ],
    )(order, flat_clips, flat_cotangent, gains, mine, theirs, early_cols)

    if split:

        def core_sum(kept, sent):
            both = widen(kept) + widen(swap(sent, "fsdp", 1))
            return both[0], both[1]

        kept_12, send_12 = core_sum(*far_sums[:2])
        send_12 = narrow(send_12)

    near_sums = call(
        rest_kernel,
        0.5,
        out_shape=shapes,
        in_specs=[vmem] * 2,
        out_specs=[vmem] * len(shapes),
        scratch_shapes=[half_weight],
    )(turned, late_cols)

    if split:
        kept_8, send_8 = core_sum(*far_sums[2:])
        kept_4, send_4 = core_sum(*near_sums[:2])
        kept_0, send_0 = core_sum(*near_sums[2:])
        send_8 = narrow(send_8)
        side_4 = swap(narrow(send_4), "fsdp", 4)
        came_12 = swap(send_12, "fsdp", 2)
        for_8 = narrow(kept_12 + widen(came_12))
        from_4 = swap(for_8, "fsdp", 4)
        for_8, send_8 = together(for_8, send_8)
        came_8 = swap(send_8, "fsdp", 2)
        ready = narrow(kept_8 + widen(came_8) + widen(from_4))
        from_8 = swap(ready, "fsdp", 8)
        send_0 = narrow(send_0 + widen(side_4))
        came_8, send_0 = together(came_8, send_0)
        came_0 = swap(send_0, "fsdp", 2)
        direct_4 = narrow(kept_4)
        from_4, direct_4 = together(from_4, direct_4)
        late = swap(direct_4, "fsdp", 4)
        weight_grad = (kept_0 + widen(came_0) + widen(late) + widen(from_8)) * factor
        grad, _ = together(grad, ready)
    else:
        summed = widen(jnp.concatenate([near_sums[0], far_sums[0]], axis=0))
        weight_grad = lax.psum_scatter(summed, "fsdp", scatter_dimension=0, tiled=True) * factor

    acts, grads = call(
        last_kernel,
        1.0,
        limit=LAST_VMEM_LIMIT,
        out_shape=[jax.ShapeDtypeStruct((1, *dims), jnp.bfloat16)] * 2,
        in_specs=[smem] + [anywhere] * 6,
        out_specs=[anywhere, anywhere],
        scratch_shapes=[
            pltpu.VMEM((all_rows, channels), jnp.bfloat16),
            pltpu.VMEM(cols_shape, jnp.bfloat16),
            clips_scratch,
            gain_scratch,
            volume_scratch,
            volume_scratch,
            pltpu.VMEM((1, *dims), jnp.bfloat16),
            pltpu.VMEM((1, *dims), jnp.bfloat16),
            pltpu.SemaphoreType.DMA((6,)),
        ],
    )(order, flat_clips, gains, hidden, grad, near_weight, far_weight)
    return (acts, grads, weight_grad[None])


def solution(mesh):
    placed = (
        P("fsdp", None, None, None, None),
        P("fsdp", None),
        P("section", None),
        P("section", "fsdp", None),
        P("fsdp", None, None, None, None),
    )
    return jax.shard_map(
        on_device,
        mesh=mesh,
        in_specs=placed,
        out_specs=(
            P("section", "fsdp", None, None, None, None),
            P("section", "fsdp", None, None, None, None),
            P("section", "fsdp", None),
        ),
        check_vma=False,
    )
```

```python
import functools
import math

import jax
import jax.numpy as jnp
from jax import lax
from jax.experimental import pallas as pl
from jax.experimental.pallas import tpu as pltpu
from jax.sharding import PartitionSpec as P

EPSILON = 1e-06
ROW_TILE = 16
VMEM_LIMIT = 20 * 1024 * 1024
LAST_VMEM_LIMIT = 24 * 1024 * 1024


def normalize(values, gain_row):
    inverse = lax.rsqrt(jnp.mean(values * values, axis=-1, keepdims=True) + EPSILON)
    return inverse, values * inverse * gain_row


def activate(values, gain_row):
    inverse, normed = normalize(values, gain_row)
    return jnp.maximum(normed, 0.0).astype(jnp.bfloat16)


def back(values, upstream, spread, gain_row):
    inverse, normed = normalize(values, gain_row)
    scaled = gain_row * jnp.where(normed > 0.0, spread, 0.0)
    mixing = jnp.mean(values * scaled, axis=-1, keepdims=True)
    return upstream + inverse * scaled - values * (inverse * inverse * inverse) * mixing


def fill_columns(cols_ref, values, dims):
    micro, frames, height, width, channels = dims
    plane = height * width
    voxels = frames * plane
    total = micro * voxels
    row = lax.broadcasted_iota(jnp.int32, (plane, channels), 0)
    across = row % width
    down = row // width
    zero = jnp.zeros((micro, plane, cols_ref.shape[2]), jnp.bfloat16)
    cols_ref[:, :plane, :] = zero
    cols_ref[:, plane + voxels :, :] = zero

    def masked(rolled, inside):
        kept = rolled.reshape(total // plane, plane, channels) * inside.astype(jnp.float32)[None]
        return kept.reshape(total, channels)

    for by_w in (-1, 0, 1):
        if by_w == 0:
            along = values
        else:
            inside = (across + by_w >= 0) & (across + by_w < width)
            along = masked(pltpu.roll(values, (-by_w) % total, 0), inside)
        for by_h in (-1, 0, 1):
            if by_h == 0:
                moved = along
            else:
                inside = (down + by_h >= 0) & (down + by_h < height)
                moved = masked(pltpu.roll(along, (-by_h * width) % total, 0), inside)
            j = 3 * (by_h + 1) + by_w + 1
            cols_ref[:, plane : plane + voxels, j * channels : (j + 1) * channels] = moved.astype(
                jnp.bfloat16
            ).reshape(micro, voxels, channels)


def frame_columns(cols_ref, by_t, dims, begin, end):
    micro, frames, height, width, channels = dims
    plane = height * width
    voxels = frames * plane
    start = plane * (by_t + 1)
    return cols_ref[:, start : start + voxels, begin:end].reshape(micro * voxels, end - begin)


def half_pieces(half, dims):
    channels = dims[4]
    middle = channels // 2
    parts = []
    at = 0
    for k in range(14) if half == 0 else range(13, 27):
        low, high = 0, channels
        if k == 13:
            low, high = (0, middle) if half == 0 else (middle, channels)
        parts.append((k, low, high, at))
        at += high - low
    return parts


def half_forward(cols_ref, weight_ref, dims, half):
    channels = dims[4]
    middle = 9 * channels // 2
    if half == 0:
        runs = ((-1, 0, 2 * middle, 0), (0, 0, middle, 2 * middle))
    else:
        runs = ((0, middle, 2 * middle, 0), (1, 0, 2 * middle, middle))
    terms = [
        jnp.dot(
            frame_columns(cols_ref, by_t, dims, begin, end),
            weight_ref[at : at + end - begin, :],
            preferred_element_type=jnp.float32,
        )
        for by_t, begin, end, at in runs
    ]
    return terms[0] + terms[1]


def half_spread(cols_ref, weight_ref, dims, half):
    channels = dims[4]
    total, partial = None, None
    for k, low, high, at in half_pieces(half, dims):
        by_t, j = (26 - k) // 9 - 1, (26 - k) % 9
        term = lax.dot_general(
            frame_columns(cols_ref, by_t, dims, j * channels, (j + 1) * channels),
            weight_ref[at : at + high - low, :],
            (((1,), (1,)), ((), ())),
            preferred_element_type=jnp.float32,
        )
        if high - low < channels:
            partial = term
        else:
            total = term if total is None else total + term
    middle = channels // 2
    if half == 0:
        return jnp.concatenate([total[:, :middle] + partial, total[:, middle:]], axis=1)
    return jnp.concatenate([total[:, :middle], total[:, middle:] + partial], axis=1)


def half_gradient(turned_ref, cols_ref, sums_ref, dims, half):
    channels = dims[4]
    for k, low, high, at in half_pieces(half, dims):
        by_t, j = (26 - k) // 9 - 1, (26 - k) % 9
        sums_ref[at : at + high - low, :] = jnp.dot(
            turned_ref[low:high, :],
            frame_columns(cols_ref, by_t, dims, j * channels, (j + 1) * channels),
            preferred_element_type=jnp.float32,
        ).astype(jnp.bfloat16)


def where_am_i(split):
    place = lax.axis_index("fsdp")
    near = place // (lax.axis_size("fsdp") // 2) if split else 0
    return lax.axis_index("section"), place, near


def lay_pieces(place, pieces, weight_ref):
    if len(pieces) == 1:
        weight_ref[...] = pieces[0][...]
        return
    for by, piece in enumerate(pieces):
        rows = piece.shape[0]
        start = pl.multiple_of(((place ^ by) % len(pieces)) * rows, ROW_TILE)
        weight_ref[pl.ds(start, rows), :] = piece[...]


def take_clips(plan_ref, clips_ref, dims):
    picked = [clips_ref[plan_ref[m]] for m in range(dims[0])]
    return jnp.concatenate(picked, axis=0).astype(jnp.float32)


def on_half(section, half, run):
    for at in (0, 1):
        for part in (0, 1):

            @pl.when((section == at) & (half == part))
            def _(at=at, part=part):
                run(at, part)


def fetch(pairs, sems):
    copies = [pltpu.make_async_copy(source, target, sems.at[at]) for at, (source, target) in enumerate(pairs)]
    for copy in copies:
        copy.start()
    return copies


def wait_all(copies):
    for copy in copies:
        copy.wait()


def prepare_kernel(dims, split, plan_ref, clips_ref, cotangent_ref, gain_ref, early_ref, cols_ref, token_ref):
    section, place, near = where_am_i(split)
    total = dims[0] * dims[1] * dims[2] * dims[3]
    active = activate(take_clips(plan_ref, clips_ref, dims), gain_ref[...])
    upstream = cotangent_ref[...].reshape(total, dims[4]).astype(jnp.float32)
    fill_columns(cols_ref, jnp.where(section == 0, active.astype(jnp.float32), upstream), dims)
    token_ref[...] = jnp.zeros_like(token_ref)


def near_kernel(dims, split, count, cols_ref, early_ref, *rest):
    pieces, (out_ref, token_ref, kept_ref, weight_ref, sems) = rest[:count], rest[count:]
    section, place, near = where_am_i(split)
    lay_pieces(place, pieces, weight_ref)
    copies = fetch([(weight_ref, kept_ref)], sems)

    def run(at, part):
        conv = half_forward if at == 0 else half_spread
        out_ref[...] = conv(cols_ref, weight_ref, dims, part)

    on_half(section, near, run)
    token_ref[...] = early_ref[...]
    wait_all(copies)


def split_gain(gain_row):
    high = gain_row.astype(jnp.bfloat16).astype(jnp.float32)
    middle = (gain_row - high).astype(jnp.bfloat16).astype(jnp.float32)
    low = gain_row - high - middle
    row = lax.broadcasted_iota(jnp.int32, (ROW_TILE, gain_row.shape[1]), 0)
    parts = jnp.where(row == 0, high, jnp.where(row == 1, middle, jnp.where(row == 2, low, 0.0)))
    return parts.astype(jnp.bfloat16)


def join_gain(parts):
    parts = parts.astype(jnp.float32)
    return (parts[0:1] + parts[1:2]) + parts[2:3]


def far_kernel(dims, split, count, plan_ref, clips_ref, gain_ref, early_ref, cols_ref, base_ref, *rest):
    pieces, (out_ref, kept_ref, weight_ref, held_ref, held_gain, sems) = rest[:count], rest[count:]
    total = base_ref.shape[0]
    section, place, near = where_am_i(split)
    arriving = fetch([(clips_ref, held_ref), (gain_ref, held_gain)], sems)
    lay_pieces(place, pieces, weight_ref)
    leaving = pltpu.make_async_copy(weight_ref, kept_ref, sems.at[2])
    leaving.start()
    wait_all(arriving)
    out_ref[total:, :] = split_gain(held_gain[...])

    def run(at, part):
        conv = half_forward if at == 0 else half_spread
        value = base_ref[...] + conv(cols_ref, weight_ref, dims, part)
        if at == 0:
            value = value + take_clips(plan_ref, held_ref, dims)
        out_ref[:total, :] = value.astype(jnp.bfloat16)

    on_half(section, 1 - near, run)
    leaving.wait()


def hand_out(place, ways, sums_ref, outs):
    if not ways:
        outs[0][...] = sums_ref[...]
        return
    rows = outs[0].shape[1]
    for at, out in enumerate(outs):
        for inner in (0, 1):
            owner = (place ^ (ways[at // 2] + at % 2 + 2 * inner)) % (sums_ref.shape[0] // rows)
            out[inner] = sums_ref[pl.ds(pl.multiple_of(owner * rows, ROW_TILE), rows), :]


def gradient_kernel(dims, split, plan_ref, clips_ref, cotangent_ref, gain_ref, mine_ref, theirs_ref,
                    early_cols_ref, grad_ref, hidden_ref, turned_ref, cols_ref, *rest):
    outs = rest[:-5]
    sums_ref, held_clips, held_cotangent, held_gain, sems = rest[-5:]
    section, place, near = where_am_i(split)
    channels = dims[4]
    total = dims[0] * dims[1] * dims[2] * dims[3]
    arriving = fetch(
        [
            (cotangent_ref, held_cotangent),
            (clips_ref, held_clips),
            (gain_ref, held_gain),
        ],
        sems,
    )
    leading = section == 0
    mine = mine_ref[:total, :].astype(jnp.float32)
    theirs = theirs_ref[:total, :].astype(jnp.float32)
    last_gain = join_gain(jnp.where(leading, theirs_ref[total:, :].astype(jnp.float32), mine_ref[total:, :].astype(jnp.float32)))
    hidden = jnp.where(leading, mine, theirs)
    spread = jnp.where(leading, theirs, mine)
    hidden_ref[...] = hidden.astype(jnp.bfloat16)
    wait_all(arriving)
    cotangent = held_cotangent[...].reshape(total, channels).astype(jnp.float32)
    upstream = back(hidden, cotangent, spread, last_gain).astype(jnp.bfloat16)
    grad_ref[...] = upstream
    unit = jnp.where(leading, take_clips(plan_ref, held_clips, dims), hidden)
    turned_ref[...] = activate(unit, held_gain[...]).T

    @pl.when(leading)
    def _():
        fill_columns(cols_ref, upstream.astype(jnp.float32), dims)

    @pl.when(jnp.logical_not(leading))
    def _():
        cols_ref[...] = early_cols_ref[...]

    for part in (0, 1):

        @pl.when(near != part)
        def _(part=part):
            half_gradient(turned_ref, cols_ref, sums_ref, dims, part)

    hand_out(place, (12, 8) if split else (), sums_ref, outs)


def rest_kernel(dims, split, turned_ref, cols_ref, *rest):
    outs, sums_ref = rest[:-1], rest[-1]
    section, place, near = where_am_i(split)
    for part in (0, 1):

        @pl.when(near == part)
        def _(part=part):
            half_gradient(turned_ref, cols_ref, sums_ref, dims, part)

    hand_out(place, (4, 0) if split else (), sums_ref, outs)


def last_kernel(dims, split, plan_ref, clips_ref, gain_ref, hidden_ref, grad_ref, near_ref, far_ref, acts_ref,
                grads_ref, weight_ref, cols_ref, held_clips, held_gain, held_hidden, held_grad, made_acts, made_grads, sems):
    section, place, near = where_am_i(split)
    half_rows = weight_ref.shape[0] // 2
    first = pl.multiple_of(near * half_rows, ROW_TILE) if split else 0
    second = pl.multiple_of((1 - near) * half_rows, ROW_TILE) if split else half_rows
    arriving = fetch(
        [
            (near_ref, weight_ref.at[pl.ds(first, half_rows)]),
            (far_ref, weight_ref.at[pl.ds(second, half_rows)]),
            (hidden_ref, held_hidden),
            (grad_ref, held_grad),
            (gain_ref, held_gain),
            (clips_ref, held_clips),
        ],
        sems,
    )
    wait_all(arriving)
    halves = weight_ref.at[pl.ds(0, half_rows)], weight_ref.at[pl.ds(half_rows, half_rows)]
    gain_row = held_gain[...]

    @pl.when(section == 0)
    def _():
        upstream = held_grad[...].astype(jnp.float32)
        fill_columns(cols_ref, upstream, dims)
        spread = half_spread(cols_ref, halves[0], dims, 0) + half_spread(cols_ref, halves[1], dims, 1)
        ordered = take_clips(plan_ref, held_clips, dims)
        back_out = back(ordered, upstream, spread, gain_row).astype(jnp.bfloat16)
        made_grads[...] = back_out.reshape(made_grads.shape)
        made_acts[...] = held_hidden[...].reshape(made_acts.shape)

    @pl.when(section != 0)
    def _():
        hidden = held_hidden[...].astype(jnp.float32)
        fill_columns(cols_ref, activate(hidden, gain_row).astype(jnp.float32), dims)
        branch = half_forward(cols_ref, halves[0], dims, 0) + half_forward(cols_ref, halves[1], dims, 1)
        made_acts[...] = (hidden + branch).astype(jnp.bfloat16).reshape(made_acts.shape)
        made_grads[...] = held_grad[...].reshape(made_grads.shape)

    wait_all(fetch([(made_acts, acts_ref), (made_grads, grads_ref)], sems))


def swap(value, axis, by):
    return lax.ppermute(value, axis, [(i, i ^ by) for i in range(lax.axis_size(axis))])


def widen(value):
    return value.astype(jnp.float32)


def narrow(value):
    return value.astype(jnp.bfloat16)


def together(*values):
    return lax.optimization_barrier(values)


def on_device(clips, plan, gains, weights, cotangent):
    peers = lax.axis_size("fsdp")
    micro, frames, height, width, channels = clips.shape
    dims = clips.shape
    voxels = frames * height * width
    total = micro * voxels
    rows = weights.shape[1]
    all_rows = rows * peers
    half_rows = all_rows // 2
    factor = 1.0 / math.sqrt(peers * total)
    order = plan[0]
    flat_clips = clips.reshape(micro, voxels, channels)
    flat_cotangent = cotangent.reshape(micro, voxels, channels)
    split = peers == 16 and rows % ROW_TILE == 0

    smem = pl.BlockSpec(memory_space=pltpu.SMEM)
    vmem = pl.BlockSpec(memory_space=pltpu.VMEM)
    anywhere = pl.BlockSpec(memory_space=pl.ANY)
    half_weight = pltpu.VMEM((half_rows, channels), jnp.bfloat16)
    clips_scratch = pltpu.VMEM((micro, voxels, channels), jnp.bfloat16)
    volume_scratch = pltpu.VMEM((total, channels), jnp.bfloat16)
    gain_scratch = pltpu.VMEM((1, channels), jnp.float32)
    cols_shape = (micro, voxels + 2 * height * width, 9 * channels)
    volume = jax.ShapeDtypeStruct((total, channels), jnp.bfloat16)
    turned_out = jax.ShapeDtypeStruct((channels, total), jnp.bfloat16)
    cols_out = jax.ShapeDtypeStruct(cols_shape, jnp.bfloat16)
    half_out = jax.ShapeDtypeStruct((half_rows, channels), jnp.bfloat16)
    token_out = jax.ShapeDtypeStruct((8, 128), jnp.float32)

    def call(kernel, share, *, limit=VMEM_LIMIT, **config):
        flops = int(2 * total * all_rows * channels * share)
        return pl.pallas_call(
            functools.partial(kernel, dims, split),
            compiler_params=pltpu.CompilerParams(vmem_limit_bytes=limit),
            cost_estimate=pl.CostEstimate(flops=flops, bytes_accessed=2 * all_rows * channels, transcendentals=0),
            **config,
        )

    own = weights[0]
    signal = gains
    if split:
        held = {0: own}
        held[2] = swap(own, "fsdp", 2)
        held[4] = swap(own, "fsdp", 4)
        held[8] = swap(own, "fsdp", 8)
        signal = held[4]

    early_cols, token = call(
        prepare_kernel,
        0.2,
        out_shape=[cols_out, token_out],
        in_specs=[smem] + [vmem] * 3 + [anywhere],
        out_specs=[vmem] * 2,
    )(order, flat_clips, flat_cotangent, gains, gains)

    if split:
        held[4], token = together(held[4], token)
        held[6] = swap(held[4], "fsdp", 2)
        held[12] = swap(held[8], "fsdp", 4)
        held[10] = swap(held[8], "fsdp", 2)
        held[14] = swap(held[12], "fsdp", 2)
        for by in (0, 2, 4, 6):
            held[by + 1] = swap(held[by], "fsdp", 1)
        near = [held[by] for by in range(8)]
    else:
        full = lax.all_gather(own, "fsdp", axis=0, tiled=True)
        near, far = [full[:half_rows]], [full[half_rows:]]
    count = len(near)

    base, token, near_weight = call(
        lambda dims, split, *refs: near_kernel(dims, split, count, *refs),
        0.5,
        out_shape=[jax.ShapeDtypeStruct((total, channels), jnp.float32), token_out, half_out],
        in_specs=[vmem] * (2 + count),
        out_specs=[vmem] * 2 + [anywhere],
        scratch_shapes=[half_weight, pltpu.SemaphoreType.DMA((1,))],
    )(early_cols, token, *near)

    if split:
        held[14], token = together(held[14], token)
        for by in (8, 10, 12, 14):
            held[by + 1] = swap(held[by], "fsdp", 1)
        far = [held[by] for by in range(8, 16)]

    mine, far_weight = call(
        lambda dims, split, *refs: far_kernel(dims, split, count, *refs),
        0.5,
        out_shape=[jax.ShapeDtypeStruct((total + ROW_TILE, channels), jnp.bfloat16), half_out],
        in_specs=[smem] + [anywhere] * 3 + [vmem] * (2 + count),
        out_specs=[vmem, anywhere],
        scratch_shapes=[half_weight, clips_scratch, gain_scratch, pltpu.SemaphoreType.DMA((3,))],
    )(order, flat_clips, gains, token, early_cols, base, *far)

    theirs = swap(mine, "section", 1)

    shapes = [jax.ShapeDtypeStruct((2, rows, channels), jnp.bfloat16)] * 4 if split else [half_out]
    grad, hidden, turned, late_cols, *far_sums = call(
        gradient_kernel,
        0.5,
        out_shape=[volume, volume, turned_out, cols_out] + shapes,
        in_specs=[smem] + [anywhere] * 3 + [vmem] * 3,
        out_specs=[vmem] * (4 + len(shapes)),
        scratch_shapes=[
            half_weight,
            clips_scratch,
            clips_scratch,
            gain_scratch,
            pltpu.SemaphoreType.DMA((3,)),
        ],
    )(order, flat_clips, flat_cotangent, gains, mine, theirs, early_cols)

    if split:

        def core_sum(kept, sent):
            both = widen(kept) + widen(swap(sent, "fsdp", 1))
            return both[0], both[1]

        cut = rows // (2 * ROW_TILE) * ROW_TILE
        parts = slice(0, cut), slice(cut, rows)
        kept_12, send_12 = core_sum(*far_sums[:2])
        send_12 = [narrow(send_12[part]) for part in parts]

    near_sums = call(
        rest_kernel,
        0.5,
        out_shape=shapes,
        in_specs=[vmem] * 2,
        out_specs=[vmem] * len(shapes),
        scratch_shapes=[half_weight],
    )(turned, late_cols)

    if split:
        kept_8, send_8 = core_sum(*far_sums[2:])
        kept_4, send_4 = core_sum(*near_sums[:2])
        kept_0, send_0 = core_sum(*near_sums[2:])
        send_8 = [narrow(send_8[part]) for part in parts]
        side_4 = swap(narrow(send_4), "fsdp", 4)
        came_12 = [swap(value, "fsdp", 2) for value in send_12]
        came_8 = []
        for at in (0, 1):
            came_12[at], send_8[at] = together(came_12[at], send_8[at])
            came_8.append(swap(send_8[at], "fsdp", 2))
        for_8 = [narrow(kept_12[part] + widen(value)) for part, value in zip(parts, came_12)]
        from_4 = [swap(value, "fsdp", 4) for value in for_8]
        ready = [
            narrow(kept_8[part] + widen(one) + widen(two)) for part, one, two in zip(parts, came_8, from_4)
        ]
        from_8 = jnp.concatenate([swap(value, "fsdp", 8) for value in ready], axis=0)
        came_0 = swap(narrow(send_0 + widen(side_4)), "fsdp", 2)
        direct_4 = narrow(kept_4)
        from_4[1], direct_4 = together(from_4[1], direct_4)
        late = swap(direct_4, "fsdp", 4)
        weight_grad = (kept_0 + widen(came_0) + widen(late) + widen(from_8)) * factor
        grad, _ = together(grad, ready[1])
    else:
        summed = widen(jnp.concatenate([near_sums[0], far_sums[0]], axis=0))
        weight_grad = lax.psum_scatter(summed, "fsdp", scatter_dimension=0, tiled=True) * factor

    acts, grads = call(
        last_kernel,
        1.0,
        limit=LAST_VMEM_LIMIT,
        out_shape=[jax.ShapeDtypeStruct((1, *dims), jnp.bfloat16)] * 2,
        in_specs=[smem] + [anywhere] * 6,
        out_specs=[anywhere, anywhere],
        scratch_shapes=[
            pltpu.VMEM((all_rows, channels), jnp.bfloat16),
            pltpu.VMEM(cols_shape, jnp.bfloat16),
            clips_scratch,
            gain_scratch,
            volume_scratch,
            volume_scratch,
            pltpu.VMEM((1, *dims), jnp.bfloat16),
            pltpu.VMEM((1, *dims), jnp.bfloat16),
            pltpu.SemaphoreType.DMA((6,)),
        ],
    )(order, flat_clips, gains, hidden, grad, near_weight, far_weight)
    return (acts, grads, weight_grad[None])


def solution(mesh):
    placed = (
        P("fsdp", None, None, None, None),
        P("fsdp", None),
        P("section", None),
        P("section", "fsdp", None),
        P("fsdp", None, None, None, None),
    )
    return jax.shard_map(
        on_device,
        mesh=mesh,
        in_specs=placed,
        out_specs=(
            P("section", "fsdp", None, None, None, None),
            P("section", "fsdp", None, None, None, None),
            P("section", "fsdp", None),
        ),
        check_vma=False,
    )
```

```python
import functools
import math

import jax
import jax.numpy as jnp
from jax import lax
from jax.experimental import pallas as pl
from jax.experimental.pallas import tpu as pltpu
from jax.sharding import PartitionSpec as P

EPSILON = 1e-06
ROW_TILE = 16
VMEM_LIMIT = 20 * 1024 * 1024
LAST_VMEM_LIMIT = 24 * 1024 * 1024


def normalize(values, gain_row):
    inverse = lax.rsqrt(jnp.mean(values * values, axis=-1, keepdims=True) + EPSILON)
    return inverse, values * inverse * gain_row


def activate(values, gain_row):
    inverse, normed = normalize(values, gain_row)
    return jnp.maximum(normed, 0.0).astype(jnp.bfloat16)


def back(values, upstream, spread, gain_row):
    inverse, normed = normalize(values, gain_row)
    scaled = gain_row * jnp.where(normed > 0.0, spread, 0.0)
    mixing = jnp.mean(values * scaled, axis=-1, keepdims=True)
    return upstream + inverse * scaled - values * (inverse * inverse * inverse) * mixing


def fill_columns(cols_ref, values, dims):
    micro, frames, height, width, channels = dims
    plane = height * width
    voxels = frames * plane
    total = micro * voxels
    row = lax.broadcasted_iota(jnp.int32, (plane, channels), 0)
    across = row % width
    down = row // width
    zero = jnp.zeros((micro, plane, cols_ref.shape[2]), jnp.bfloat16)
    cols_ref[:, :plane, :] = zero
    cols_ref[:, plane + voxels :, :] = zero

    def masked(rolled, inside):
        kept = rolled.reshape(total // plane, plane, channels) * inside.astype(jnp.float32)[None]
        return kept.reshape(total, channels)

    for by_w in (-1, 0, 1):
        if by_w == 0:
            along = values
        else:
            inside = (across + by_w >= 0) & (across + by_w < width)
            along = masked(pltpu.roll(values, (-by_w) % total, 0), inside)
        for by_h in (-1, 0, 1):
            if by_h == 0:
                moved = along
            else:
                inside = (down + by_h >= 0) & (down + by_h < height)
                moved = masked(pltpu.roll(along, (-by_h * width) % total, 0), inside)
            j = 3 * (by_h + 1) + by_w + 1
            cols_ref[:, plane : plane + voxels, j * channels : (j + 1) * channels] = moved.astype(
                jnp.bfloat16
            ).reshape(micro, voxels, channels)


def frame_columns(cols_ref, by_t, dims, begin, end):
    micro, frames, height, width, channels = dims
    plane = height * width
    voxels = frames * plane
    start = plane * (by_t + 1)
    return cols_ref[:, start : start + voxels, begin:end].reshape(micro * voxels, end - begin)


def half_pieces(half, dims):
    channels = dims[4]
    middle = channels // 2
    parts = []
    at = 0
    for k in range(14) if half == 0 else range(13, 27):
        low, high = 0, channels
        if k == 13:
            low, high = (0, middle) if half == 0 else (middle, channels)
        parts.append((k, low, high, at))
        at += high - low
    return parts


def half_forward(cols_ref, weight_ref, dims, half):
    channels = dims[4]
    middle = 9 * channels // 2
    if half == 0:
        runs = ((-1, 0, 2 * middle, 0), (0, 0, middle, 2 * middle))
    else:
        runs = ((0, middle, 2 * middle, 0), (1, 0, 2 * middle, middle))
    terms = [
        jnp.dot(
            frame_columns(cols_ref, by_t, dims, begin, end),
            weight_ref[at : at + end - begin, :],
            preferred_element_type=jnp.float32,
        )
        for by_t, begin, end, at in runs
    ]
    return terms[0] + terms[1]


def half_spread(cols_ref, weight_ref, dims, half):
    channels = dims[4]
    total, partial = None, None
    for k, low, high, at in half_pieces(half, dims):
        by_t, j = (26 - k) // 9 - 1, (26 - k) % 9
        term = lax.dot_general(
            frame_columns(cols_ref, by_t, dims, j * channels, (j + 1) * channels),
            weight_ref[at : at + high - low, :],
            (((1,), (1,)), ((), ())),
            preferred_element_type=jnp.float32,
        )
        if high - low < channels:
            partial = term
        else:
            total = term if total is None else total + term
    middle = channels // 2
    if half == 0:
        return jnp.concatenate([total[:, :middle] + partial, total[:, middle:]], axis=1)
    return jnp.concatenate([total[:, :middle], total[:, middle:] + partial], axis=1)


def half_gradient(turned_ref, cols_ref, sums_ref, dims, half):
    channels = dims[4]
    for k, low, high, at in half_pieces(half, dims):
        by_t, j = (26 - k) // 9 - 1, (26 - k) % 9
        sums_ref[at : at + high - low, :] = jnp.dot(
            turned_ref[low:high, :],
            frame_columns(cols_ref, by_t, dims, j * channels, (j + 1) * channels),
            preferred_element_type=jnp.float32,
        ).astype(jnp.bfloat16)


def where_am_i(split):
    place = lax.axis_index("fsdp")
    near = place // (lax.axis_size("fsdp") // 2) if split else 0
    return lax.axis_index("section"), place, near


def lay_pieces(place, pieces, weight_ref):
    if len(pieces) == 1:
        weight_ref[...] = pieces[0][...]
        return
    for by, piece in enumerate(pieces):
        rows = piece.shape[0]
        start = pl.multiple_of(((place ^ by) % len(pieces)) * rows, ROW_TILE)
        weight_ref[pl.ds(start, rows), :] = piece[...]


def take_clips(plan_ref, clips_ref, dims):
    picked = [clips_ref[plan_ref[m]] for m in range(dims[0])]
    return jnp.concatenate(picked, axis=0).astype(jnp.float32)


def on_half(section, half, run):
    for at in (0, 1):
        for part in (0, 1):

            @pl.when((section == at) & (half == part))
            def _(at=at, part=part):
                run(at, part)


def fetch(pairs, sems):
    copies = [pltpu.make_async_copy(source, target, sems.at[at]) for at, (source, target) in enumerate(pairs)]
    for copy in copies:
        copy.start()
    return copies


def wait_all(copies):
    for copy in copies:
        copy.wait()


def prepare_kernel(dims, split, plan_ref, clips_ref, cotangent_ref, gain_ref, early_ref, cols_ref, token_ref):
    section, place, near = where_am_i(split)
    total = dims[0] * dims[1] * dims[2] * dims[3]
    active = activate(take_clips(plan_ref, clips_ref, dims), gain_ref[...])
    upstream = cotangent_ref[...].reshape(total, dims[4]).astype(jnp.float32)
    fill_columns(cols_ref, jnp.where(section == 0, active.astype(jnp.float32), upstream), dims)
    token_ref[...] = jnp.zeros_like(token_ref)


def near_kernel(dims, split, count, cols_ref, early_ref, *rest):
    pieces, (out_ref, token_ref, kept_ref, weight_ref, sems) = rest[:count], rest[count:]
    section, place, near = where_am_i(split)
    lay_pieces(place, pieces, weight_ref)
    copies = fetch([(weight_ref, kept_ref)], sems)

    def run(at, part):
        conv = half_forward if at == 0 else half_spread
        out_ref[...] = conv(cols_ref, weight_ref, dims, part)

    on_half(section, near, run)
    token_ref[...] = early_ref[...]
    wait_all(copies)


def split_gain(gain_row):
    high = gain_row.astype(jnp.bfloat16).astype(jnp.float32)
    middle = (gain_row - high).astype(jnp.bfloat16).astype(jnp.float32)
    low = gain_row - high - middle
    row = lax.broadcasted_iota(jnp.int32, (ROW_TILE, gain_row.shape[1]), 0)
    parts = jnp.where(row == 0, high, jnp.where(row == 1, middle, jnp.where(row == 2, low, 0.0)))
    return parts.astype(jnp.bfloat16)


def join_gain(parts):
    parts = parts.astype(jnp.float32)
    return (parts[0:1] + parts[1:2]) + parts[2:3]


def far_kernel(dims, split, count, plan_ref, clips_ref, gain_ref, early_ref, cols_ref, base_ref, *rest):
    pieces, (out_ref, kept_ref, weight_ref, held_ref, held_gain, sems) = rest[:count], rest[count:]
    total = base_ref.shape[0]
    section, place, near = where_am_i(split)
    arriving = fetch([(clips_ref, held_ref), (gain_ref, held_gain)], sems)
    lay_pieces(place, pieces, weight_ref)
    leaving = pltpu.make_async_copy(weight_ref, kept_ref, sems.at[2])
    leaving.start()
    wait_all(arriving)
    out_ref[total:, :] = split_gain(held_gain[...])

    def run(at, part):
        conv = half_forward if at == 0 else half_spread
        value = base_ref[...] + conv(cols_ref, weight_ref, dims, part)
        if at == 0:
            value = value + take_clips(plan_ref, held_ref, dims)
        out_ref[:total, :] = value.astype(jnp.bfloat16)

    on_half(section, 1 - near, run)
    leaving.wait()


def hand_out(place, ways, sums_ref, outs):
    if not ways:
        outs[0][...] = sums_ref[...]
        return
    rows = outs[0].shape[1]
    for at, out in enumerate(outs):
        for inner in (0, 1):
            owner = (place ^ (ways[at // 2] + at % 2 + 2 * inner)) % (sums_ref.shape[0] // rows)
            out[inner] = sums_ref[pl.ds(pl.multiple_of(owner * rows, ROW_TILE), rows), :]


def gradient_kernel(dims, split, plan_ref, clips_ref, cotangent_ref, gain_ref, mine_ref, theirs_ref,
                    early_cols_ref, grad_ref, hidden_ref, turned_ref, cols_ref, *rest):
    outs = rest[:-5]
    sums_ref, held_clips, held_cotangent, held_gain, sems = rest[-5:]
    section, place, near = where_am_i(split)
    channels = dims[4]
    total = dims[0] * dims[1] * dims[2] * dims[3]
    arriving = fetch(
        [
            (cotangent_ref, held_cotangent),
            (clips_ref, held_clips),
            (gain_ref, held_gain),
        ],
        sems,
    )
    leading = section == 0
    mine = mine_ref[:total, :].astype(jnp.float32)
    theirs = theirs_ref[:total, :].astype(jnp.float32)
    last_gain = join_gain(jnp.where(leading, theirs_ref[total:, :].astype(jnp.float32), mine_ref[total:, :].astype(jnp.float32)))
    hidden = jnp.where(leading, mine, theirs)
    spread = jnp.where(leading, theirs, mine)
    hidden_ref[...] = hidden.astype(jnp.bfloat16)
    wait_all(arriving)
    cotangent = held_cotangent[...].reshape(total, channels).astype(jnp.float32)
    upstream = back(hidden, cotangent, spread, last_gain).astype(jnp.bfloat16)
    grad_ref[...] = upstream
    unit = jnp.where(leading, take_clips(plan_ref, held_clips, dims), hidden)
    turned_ref[...] = activate(unit, held_gain[...]).T

    @pl.when(leading)
    def _():
        fill_columns(cols_ref, upstream.astype(jnp.float32), dims)

    @pl.when(jnp.logical_not(leading))
    def _():
        cols_ref[...] = early_cols_ref[...]

    for part in (0, 1):

        @pl.when(near != part)
        def _(part=part):
            half_gradient(turned_ref, cols_ref, sums_ref, dims, part)

    hand_out(place, (12, 8) if split else (), sums_ref, outs)


def rest_kernel(dims, split, turned_ref, cols_ref, *rest):
    outs, sums_ref = rest[:-1], rest[-1]
    section, place, near = where_am_i(split)
    for part in (0, 1):

        @pl.when(near == part)
        def _(part=part):
            half_gradient(turned_ref, cols_ref, sums_ref, dims, part)

    hand_out(place, (4, 0) if split else (), sums_ref, outs)


def last_kernel(dims, split, plan_ref, clips_ref, gain_ref, hidden_ref, grad_ref, near_ref, far_ref, acts_ref,
                grads_ref, weight_ref, cols_ref, held_clips, held_gain, held_hidden, held_grad, made_acts, made_grads, sems):
    section, place, near = where_am_i(split)
    half_rows = weight_ref.shape[0] // 2
    first = pl.multiple_of(near * half_rows, ROW_TILE) if split else 0
    second = pl.multiple_of((1 - near) * half_rows, ROW_TILE) if split else half_rows
    arriving = fetch(
        [
            (near_ref, weight_ref.at[pl.ds(first, half_rows)]),
            (far_ref, weight_ref.at[pl.ds(second, half_rows)]),
            (hidden_ref, held_hidden),
            (grad_ref, held_grad),
            (gain_ref, held_gain),
            (clips_ref, held_clips),
        ],
        sems,
    )
    wait_all(arriving)
    halves = weight_ref.at[pl.ds(0, half_rows)], weight_ref.at[pl.ds(half_rows, half_rows)]
    gain_row = held_gain[...]

    @pl.when(section == 0)
    def _():
        upstream = held_grad[...].astype(jnp.float32)
        fill_columns(cols_ref, upstream, dims)
        spread = half_spread(cols_ref, halves[0], dims, 0) + half_spread(cols_ref, halves[1], dims, 1)
        ordered = take_clips(plan_ref, held_clips, dims)
        back_out = back(ordered, upstream, spread, gain_row).astype(jnp.bfloat16)
        made_grads[...] = back_out.reshape(made_grads.shape)
        made_acts[...] = held_hidden[...].reshape(made_acts.shape)

    @pl.when(section != 0)
    def _():
        hidden = held_hidden[...].astype(jnp.float32)
        fill_columns(cols_ref, activate(hidden, gain_row).astype(jnp.float32), dims)
        branch = half_forward(cols_ref, halves[0], dims, 0) + half_forward(cols_ref, halves[1], dims, 1)
        made_acts[...] = (hidden + branch).astype(jnp.bfloat16).reshape(made_acts.shape)
        made_grads[...] = held_grad[...].reshape(made_grads.shape)

    wait_all(fetch([(made_acts, acts_ref), (made_grads, grads_ref)], sems))


def swap(value, axis, by):
    return lax.ppermute(value, axis, [(i, i ^ by) for i in range(lax.axis_size(axis))])


def widen(value):
    return value.astype(jnp.float32)


def narrow(value):
    return value.astype(jnp.bfloat16)


def together(*values):
    return lax.optimization_barrier(values)


def on_device(clips, plan, gains, weights, cotangent):
    peers = lax.axis_size("fsdp")
    micro, frames, height, width, channels = clips.shape
    dims = clips.shape
    voxels = frames * height * width
    total = micro * voxels
    rows = weights.shape[1]
    all_rows = rows * peers
    half_rows = all_rows // 2
    factor = 1.0 / math.sqrt(peers * total)
    order = plan[0]
    flat_clips = clips.reshape(micro, voxels, channels)
    flat_cotangent = cotangent.reshape(micro, voxels, channels)
    split = peers == 16 and rows % ROW_TILE == 0

    smem = pl.BlockSpec(memory_space=pltpu.SMEM)
    vmem = pl.BlockSpec(memory_space=pltpu.VMEM)
    anywhere = pl.BlockSpec(memory_space=pl.ANY)
    half_weight = pltpu.VMEM((half_rows, channels), jnp.bfloat16)
    clips_scratch = pltpu.VMEM((micro, voxels, channels), jnp.bfloat16)
    volume_scratch = pltpu.VMEM((total, channels), jnp.bfloat16)
    gain_scratch = pltpu.VMEM((1, channels), jnp.float32)
    cols_shape = (micro, voxels + 2 * height * width, 9 * channels)
    volume = jax.ShapeDtypeStruct((total, channels), jnp.bfloat16)
    turned_out = jax.ShapeDtypeStruct((channels, total), jnp.bfloat16)
    cols_out = jax.ShapeDtypeStruct(cols_shape, jnp.bfloat16)
    half_out = jax.ShapeDtypeStruct((half_rows, channels), jnp.bfloat16)
    token_out = jax.ShapeDtypeStruct((8, 128), jnp.float32)

    def call(kernel, share, *, limit=VMEM_LIMIT, **config):
        flops = int(2 * total * all_rows * channels * share)
        return pl.pallas_call(
            functools.partial(kernel, dims, split),
            compiler_params=pltpu.CompilerParams(vmem_limit_bytes=limit),
            cost_estimate=pl.CostEstimate(flops=flops, bytes_accessed=2 * all_rows * channels, transcendentals=0),
            **config,
        )

    own = weights[0]
    signal = gains
    if split:
        held = {0: own}
        held[2] = swap(own, "fsdp", 2)
        held[4] = swap(own, "fsdp", 4)
        held[8] = swap(own, "fsdp", 8)
        signal = held[4]

    early_cols, token = call(
        prepare_kernel,
        0.2,
        out_shape=[cols_out, token_out],
        in_specs=[smem] + [vmem] * 3 + [anywhere],
        out_specs=[vmem] * 2,
    )(order, flat_clips, flat_cotangent, gains, gains)

    if split:
        held[4], token = together(held[4], token)
        held[6] = swap(held[4], "fsdp", 2)
        held[12] = swap(held[8], "fsdp", 4)
        held[10] = swap(held[8], "fsdp", 2)
        held[14] = swap(held[12], "fsdp", 2)
        for by in (0, 2, 4, 6):
            held[by + 1] = swap(held[by], "fsdp", 1)
        near = [held[by] for by in range(8)]
    else:
        full = lax.all_gather(own, "fsdp", axis=0, tiled=True)
        near, far = [full[:half_rows]], [full[half_rows:]]
    count = len(near)

    base, token, near_weight = call(
        lambda dims, split, *refs: near_kernel(dims, split, count, *refs),
        0.5,
        out_shape=[jax.ShapeDtypeStruct((total, channels), jnp.float32), token_out, half_out],
        in_specs=[vmem] * (2 + count),
        out_specs=[vmem] * 2 + [anywhere],
        scratch_shapes=[half_weight, pltpu.SemaphoreType.DMA((1,))],
    )(early_cols, token, *near)

    if split:
        held[14], token = together(held[14], token)
        for by in (8, 10, 12, 14):
            held[by + 1] = swap(held[by], "fsdp", 1)
        far = [held[by] for by in range(8, 16)]

    mine, far_weight = call(
        lambda dims, split, *refs: far_kernel(dims, split, count, *refs),
        0.5,
        out_shape=[jax.ShapeDtypeStruct((total + ROW_TILE, channels), jnp.bfloat16), half_out],
        in_specs=[smem] + [anywhere] * 3 + [vmem] * (2 + count),
        out_specs=[vmem, anywhere],
        scratch_shapes=[half_weight, clips_scratch, gain_scratch, pltpu.SemaphoreType.DMA((3,))],
    )(order, flat_clips, gains, token, early_cols, base, *far)

    theirs = swap(mine, "section", 1)

    shapes = [jax.ShapeDtypeStruct((2, rows, channels), jnp.bfloat16)] * 4 if split else [half_out]
    grad, hidden, turned, late_cols, *far_sums = call(
        gradient_kernel,
        0.5,
        out_shape=[volume, volume, turned_out, cols_out] + shapes,
        in_specs=[smem] + [anywhere] * 3 + [vmem] * 3,
        out_specs=[vmem] * (4 + len(shapes)),
        scratch_shapes=[
            half_weight,
            clips_scratch,
            clips_scratch,
            gain_scratch,
            pltpu.SemaphoreType.DMA((3,)),
        ],
    )(order, flat_clips, flat_cotangent, gains, mine, theirs, early_cols)

    if split:

        def core_sum(kept, sent):
            both = widen(kept) + widen(swap(sent, "fsdp", 1))
            return both[0], both[1]

        cut = rows // (2 * ROW_TILE) * ROW_TILE
        parts = slice(0, cut), slice(cut, rows)
        kept_12, send_12 = core_sum(*far_sums[:2])
        send_12 = [narrow(send_12[part]) for part in parts]

    near_sums = call(
        rest_kernel,
        0.5,
        out_shape=shapes,
        in_specs=[vmem] * 2,
        out_specs=[vmem] * len(shapes),
        scratch_shapes=[half_weight],
    )(turned, late_cols)

    if split:
        kept_8, send_8 = core_sum(*far_sums[2:])
        kept_4, send_4 = core_sum(*near_sums[:2])
        kept_0, send_0 = core_sum(*near_sums[2:])
        send_8 = [narrow(send_8[part]) for part in parts]
        side_4 = swap(narrow(send_4), "fsdp", 4)
        came_12 = [swap(value, "fsdp", 2) for value in send_12]
        came_8 = []
        for at in (0, 1):
            came_12[at], send_8[at] = together(came_12[at], send_8[at])
            came_8.append(swap(send_8[at], "fsdp", 2))
        for_8 = [narrow(kept_12[part] + widen(value)) for part, value in zip(parts, came_12)]
        from_4 = [swap(value, "fsdp", 4) for value in for_8]
        ready = [
            narrow(kept_8[part] + widen(one) + widen(two)) for part, one, two in zip(parts, came_8, from_4)
        ]
        from_8 = jnp.concatenate([swap(value, "fsdp", 8) for value in ready], axis=0)
        came_0 = swap(narrow(send_0 + widen(side_4)), "fsdp", 2)
        direct_4 = narrow(kept_4)
        from_4[0], direct_4 = together(from_4[0], direct_4)
        late = swap(direct_4, "fsdp", 4)
        weight_grad = (kept_0 + widen(came_0) + widen(late) + widen(from_8)) * factor
        grad, _ = together(grad, ready[1])
    else:
        summed = widen(jnp.concatenate([near_sums[0], far_sums[0]], axis=0))
        weight_grad = lax.psum_scatter(summed, "fsdp", scatter_dimension=0, tiled=True) * factor

    acts, grads = call(
        last_kernel,
        1.0,
        limit=LAST_VMEM_LIMIT,
        out_shape=[jax.ShapeDtypeStruct((1, *dims), jnp.bfloat16)] * 2,
        in_specs=[smem] + [anywhere] * 6,
        out_specs=[anywhere, anywhere],
        scratch_shapes=[
            pltpu.VMEM((all_rows, channels), jnp.bfloat16),
            pltpu.VMEM(cols_shape, jnp.bfloat16),
            clips_scratch,
            gain_scratch,
            volume_scratch,
            volume_scratch,
            pltpu.VMEM((1, *dims), jnp.bfloat16),
            pltpu.VMEM((1, *dims), jnp.bfloat16),
            pltpu.SemaphoreType.DMA((6,)),
        ],
    )(order, flat_clips, gains, hidden, grad, near_weight, far_weight)
    return (acts, grads, weight_grad[None])


def solution(mesh):
    placed = (
        P("fsdp", None, None, None, None),
        P("fsdp", None),
        P("section", None),
        P("section", "fsdp", None),
        P("fsdp", None, None, None, None),
    )
    return jax.shard_map(
        on_device,
        mesh=mesh,
        in_specs=placed,
        out_specs=(
            P("section", "fsdp", None, None, None, None),
            P("section", "fsdp", None, None, None, None),
            P("section", "fsdp", None),
        ),
        check_vma=False,
    )
```

```python
import functools
import math

import jax
import jax.numpy as jnp
from jax import lax
from jax.experimental import pallas as pl
from jax.experimental.pallas import tpu as pltpu
from jax.sharding import PartitionSpec as P

EPSILON = 1e-06
ROW_TILE = 16
VMEM_LIMIT = 20 * 1024 * 1024
LAST_VMEM_LIMIT = 24 * 1024 * 1024


def normalize(values, gain_row):
    inverse = lax.rsqrt(jnp.mean(values * values, axis=-1, keepdims=True) + EPSILON)
    return inverse, values * inverse * gain_row


def activate(values, gain_row):
    inverse, normed = normalize(values, gain_row)
    return jnp.maximum(normed, 0.0).astype(jnp.bfloat16)


def back(values, upstream, spread, gain_row):
    inverse, normed = normalize(values, gain_row)
    scaled = gain_row * jnp.where(normed > 0.0, spread, 0.0)
    mixing = jnp.mean(values * scaled, axis=-1, keepdims=True)
    return upstream + inverse * scaled - values * (inverse * inverse * inverse) * mixing


def fill_columns(cols_ref, values, dims):
    micro, frames, height, width, channels = dims
    plane = height * width
    voxels = frames * plane
    total = micro * voxels
    row = lax.broadcasted_iota(jnp.int32, (plane, channels), 0)
    across = row % width
    down = row // width
    zero = jnp.zeros((micro, plane, cols_ref.shape[2]), jnp.bfloat16)
    cols_ref[:, :plane, :] = zero
    cols_ref[:, plane + voxels :, :] = zero

    def masked(rolled, inside):
        kept = rolled.reshape(total // plane, plane, channels) * inside.astype(jnp.float32)[None]
        return kept.reshape(total, channels)

    for by_w in (-1, 0, 1):
        if by_w == 0:
            along = values
        else:
            inside = (across + by_w >= 0) & (across + by_w < width)
            along = masked(pltpu.roll(values, (-by_w) % total, 0), inside)
        for by_h in (-1, 0, 1):
            if by_h == 0:
                moved = along
            else:
                inside = (down + by_h >= 0) & (down + by_h < height)
                moved = masked(pltpu.roll(along, (-by_h * width) % total, 0), inside)
            j = 3 * (by_h + 1) + by_w + 1
            cols_ref[:, plane : plane + voxels, j * channels : (j + 1) * channels] = moved.astype(
                jnp.bfloat16
            ).reshape(micro, voxels, channels)


def frame_columns(cols_ref, by_t, dims, begin, end):
    micro, frames, height, width, channels = dims
    plane = height * width
    voxels = frames * plane
    start = plane * (by_t + 1)
    return cols_ref[:, start : start + voxels, begin:end].reshape(micro * voxels, end - begin)


def half_pieces(half, dims):
    channels = dims[4]
    middle = channels // 2
    parts = []
    at = 0
    for k in range(14) if half == 0 else range(13, 27):
        low, high = 0, channels
        if k == 13:
            low, high = (0, middle) if half == 0 else (middle, channels)
        parts.append((k, low, high, at))
        at += high - low
    return parts


def half_forward(cols_ref, weight_ref, dims, half):
    channels = dims[4]
    middle = 9 * channels // 2
    if half == 0:
        runs = ((-1, 0, 2 * middle, 0), (0, 0, middle, 2 * middle))
    else:
        runs = ((0, middle, 2 * middle, 0), (1, 0, 2 * middle, middle))
    terms = [
        jnp.dot(
            frame_columns(cols_ref, by_t, dims, begin, end),
            weight_ref[at : at + end - begin, :],
            preferred_element_type=jnp.float32,
        )
        for by_t, begin, end, at in runs
    ]
    return terms[0] + terms[1]


def half_spread(cols_ref, weight_ref, dims, half):
    channels = dims[4]
    total, partial = None, None
    for k, low, high, at in half_pieces(half, dims):
        by_t, j = (26 - k) // 9 - 1, (26 - k) % 9
        term = lax.dot_general(
            frame_columns(cols_ref, by_t, dims, j * channels, (j + 1) * channels),
            weight_ref[at : at + high - low, :],
            (((1,), (1,)), ((), ())),
            preferred_element_type=jnp.float32,
        )
        if high - low < channels:
            partial = term
        else:
            total = term if total is None else total + term
    middle = channels // 2
    if half == 0:
        return jnp.concatenate([total[:, :middle] + partial, total[:, middle:]], axis=1)
    return jnp.concatenate([total[:, :middle], total[:, middle:] + partial], axis=1)


def half_gradient(turned_refs, cols_refs, sums_ref, dims, half):
    channels = dims[4]
    for k, low, high, at in half_pieces(half, dims):
        by_t, j = (26 - k) // 9 - 1, (26 - k) % 9
        total = None
        for turned_ref, cols_ref in zip(turned_refs, cols_refs):
            some = (cols_ref.shape[0], *dims[1:])
            term = jnp.dot(
                turned_ref[low:high, :],
                frame_columns(cols_ref, by_t, some, j * channels, (j + 1) * channels),
                preferred_element_type=jnp.float32,
            )
            total = term if total is None else total + term
        sums_ref[at : at + high - low, :] = total.astype(jnp.bfloat16)


def where_am_i(split):
    place = lax.axis_index("fsdp")
    near = place // (lax.axis_size("fsdp") // 2) if split else 0
    return lax.axis_index("section"), place, near


def lay_pieces(place, pieces, weight_ref):
    if len(pieces) == 1:
        weight_ref[...] = pieces[0][...]
        return
    for by, piece in enumerate(pieces):
        rows = piece.shape[0]
        start = pl.multiple_of(((place ^ by) % len(pieces)) * rows, ROW_TILE)
        weight_ref[pl.ds(start, rows), :] = piece[...]


def take_clips(plan_ref, clips_ref, dims):
    picked = [clips_ref[plan_ref[m]] for m in range(dims[0])]
    return jnp.concatenate(picked, axis=0).astype(jnp.float32)


def on_half(section, half, run):
    for at in (0, 1):
        for part in (0, 1):

            @pl.when((section == at) & (half == part))
            def _(at=at, part=part):
                run(at, part)


def fetch(pairs, sems):
    copies = [pltpu.make_async_copy(source, target, sems.at[at]) for at, (source, target) in enumerate(pairs)]
    for copy in copies:
        copy.start()
    return copies


def wait_all(copies):
    for copy in copies:
        copy.wait()


def prepare_kernel(dims, split, plan_ref, clips_ref, cotangent_ref, gain_ref, early_ref, cols_ref, token_ref):
    section, place, near = where_am_i(split)
    total = dims[0] * dims[1] * dims[2] * dims[3]
    active = activate(take_clips(plan_ref, clips_ref, dims), gain_ref[...])
    upstream = cotangent_ref[...].reshape(total, dims[4]).astype(jnp.float32)
    fill_columns(cols_ref, jnp.where(section == 0, active.astype(jnp.float32), upstream), dims)
    token_ref[...] = jnp.zeros_like(token_ref)


def near_kernel(dims, split, count, cols_ref, early_ref, *rest):
    pieces, (out_ref, token_ref, kept_ref, weight_ref, sems) = rest[:count], rest[count:]
    section, place, near = where_am_i(split)
    lay_pieces(place, pieces, weight_ref)
    copies = fetch([(weight_ref, kept_ref)], sems)

    def run(at, part):
        conv = half_forward if at == 0 else half_spread
        out_ref[...] = conv(cols_ref, weight_ref, dims, part)

    on_half(section, near, run)
    token_ref[...] = early_ref[...]
    wait_all(copies)


def split_gain(gain_row):
    high = gain_row.astype(jnp.bfloat16).astype(jnp.float32)
    middle = (gain_row - high).astype(jnp.bfloat16).astype(jnp.float32)
    low = gain_row - high - middle
    row = lax.broadcasted_iota(jnp.int32, (ROW_TILE, gain_row.shape[1]), 0)
    parts = jnp.where(row == 0, high, jnp.where(row == 1, middle, jnp.where(row == 2, low, 0.0)))
    return parts.astype(jnp.bfloat16)


def join_gain(parts):
    parts = parts.astype(jnp.float32)
    return (parts[0:1] + parts[1:2]) + parts[2:3]


def far_kernel(dims, split, count, plan_ref, clips_ref, gain_ref, early_ref, cols_ref, base_ref, *rest):
    pieces, (out_ref, weight_ref, held_ref, held_gain, sems) = rest[:count], rest[count:]
    arriving = fetch([(clips_ref, held_ref), (gain_ref, held_gain)], sems)
    lay_pieces(lax.axis_index("fsdp"), pieces, weight_ref)
    wait_all(arriving)
    rows = out_ref.shape[0] - ROW_TILE
    out_ref[rows:, :] = split_gain(held_gain[...])
    finish_clips(dims, split, 0, plan_ref, held_ref, cols_ref, base_ref, weight_ref, out_ref)


def other_kernel(dims, split, plan_ref, clips_ref, cols_ref, base_ref, weight_ref, out_ref, held_ref, sems):
    wait_all(fetch([(clips_ref, held_ref)], sems))
    finish_clips(dims, split, dims[0] // 2, plan_ref, held_ref, cols_ref, base_ref, weight_ref, out_ref)


def finish_clips(dims, split, first, plan_ref, clips_ref, cols_ref, base_ref, weight_ref, out_ref):
    section, place, near = where_am_i(split)
    voxels = dims[1] * dims[2] * dims[3]
    last = dims[0] // 2 if first == 0 else dims[0]
    rows = (last - first) * voxels
    some = (last - first, *dims[1:])

    def run(at, part):
        conv = half_forward if at == 0 else half_spread
        value = base_ref[first * voxels : last * voxels, :] + conv(cols_ref.at[first:last], weight_ref, some, part)
        if at == 0:
            picked = [clips_ref[plan_ref[m]].astype(jnp.float32) for m in range(first, last)]
            value = value + jnp.concatenate(picked, axis=0)
        out_ref[:rows, :] = value.astype(jnp.bfloat16)

    on_half(section, 1 - near, run)


def hand_out(place, ways, sums_ref, outs):
    if not ways:
        outs[0][...] = sums_ref[...]
        return
    rows = outs[0].shape[1]
    for at, out in enumerate(outs):
        for inner in (0, 1):
            owner = (place ^ (ways[at // 2] + at % 2 + 2 * inner)) % (sums_ref.shape[0] // rows)
            out[inner] = sums_ref[pl.ds(pl.multiple_of(owner * rows, ROW_TILE), rows), :]


def prelude(dims, split, first, plan_ref, clips_ref, cotangent_ref, gain_row, gains_refs, mine, theirs,
            early_cols_ref, grad_ref, hidden_ref, turned_ref, cols_ref):
    section, place, near = where_am_i(split)
    leading = section == 0
    last = dims[0] // 2 if first == 0 else dims[0]
    mine, theirs = mine.astype(jnp.float32), theirs.astype(jnp.float32)
    hidden = jnp.where(leading, mine, theirs)
    spread = jnp.where(leading, theirs, mine)
    last_gain = jnp.where(leading, join_gain(gains_refs[1][...]), join_gain(gains_refs[0][...]))
    cotangent = cotangent_ref[first:last].reshape(hidden.shape).astype(jnp.float32)
    upstream = back(hidden, cotangent, spread, last_gain).astype(jnp.bfloat16)
    grad_ref[...] = upstream
    hidden_ref[...] = hidden.astype(jnp.bfloat16)
    picked = jnp.concatenate([clips_ref[plan_ref[m]] for m in range(first, last)], axis=0).astype(jnp.float32)
    turned_ref[...] = activate(jnp.where(leading, picked, hidden), gain_row).T

    @pl.when(leading)
    def _():
        fill_columns(cols_ref, upstream.astype(jnp.float32), (last - first, *dims[1:]))

    @pl.when(jnp.logical_not(leading))
    def _():
        cols_ref[...] = early_cols_ref[first:last]


def begin_kernel(dims, split, plan_ref, clips_ref, cotangent_ref, gain_ref, mine_ref, theirs_ref, early_cols_ref,
                 grad_ref, hidden_ref, turned_ref, cols_ref, held_clips, held_cotangent, held_gain, sems):
    wait_all(fetch([(cotangent_ref, held_cotangent), (clips_ref, held_clips), (gain_ref, held_gain)], sems))
    rows = grad_ref.shape[0]
    gains_refs = mine_ref.at[rows : rows + ROW_TILE], theirs_ref.at[rows : rows + ROW_TILE]
    prelude(dims, split, 0, plan_ref, held_clips, held_cotangent, held_gain[...], gains_refs, mine_ref[:rows, :],
            theirs_ref[:rows, :], early_cols_ref, grad_ref, hidden_ref, turned_ref, cols_ref)


def gradient_kernel(dims, split, plan_ref, clips_ref, cotangent_ref, gain_ref, mine_ref, theirs_ref, other_mine_ref,
                    other_theirs_ref, early_cols_ref, first_turned_ref, first_cols_ref, grad_ref, hidden_ref,
                    turned_ref, cols_ref, *rest):
    outs = rest[:-5]
    sums_ref, held_clips, held_cotangent, held_gain, sems = rest[-5:]
    wait_all(fetch([(cotangent_ref, held_cotangent), (clips_ref, held_clips), (gain_ref, held_gain)], sems))
    section, place, near = where_am_i(split)
    rows = mine_ref.shape[0] - ROW_TILE
    gains_refs = mine_ref.at[rows : rows + ROW_TILE], theirs_ref.at[rows : rows + ROW_TILE]
    prelude(dims, split, dims[0] // 2, plan_ref, held_clips, held_cotangent, held_gain[...], gains_refs,
            other_mine_ref[...], other_theirs_ref[...], early_cols_ref, grad_ref, hidden_ref, turned_ref, cols_ref)
    for part in (0, 1):

        @pl.when(near != part)
        def _(part=part):
            half_gradient((first_turned_ref, turned_ref), (first_cols_ref, cols_ref), sums_ref, dims, part)

    hand_out(place, (12, 8) if split else (), sums_ref, outs)


def rest_kernel(dims, split, first_turned_ref, first_cols_ref, turned_ref, cols_ref, *rest):
    outs, sums_ref = rest[:-1], rest[-1]
    section, place, near = where_am_i(split)
    for part in (0, 1):

        @pl.when(near == part)
        def _(part=part):
            half_gradient((first_turned_ref, turned_ref), (first_cols_ref, cols_ref), sums_ref, dims, part)

    hand_out(place, (4, 0) if split else (), sums_ref, outs)


def last_kernel(dims, split, plan_ref, clips_ref, gain_ref, hidden_ref, grad_ref, other_hidden_ref, other_grad_ref,
                near_ref, far_ref, acts_ref, grads_ref, cols_ref, held_clips, held_gain, held_hidden, held_grad,
                made_acts, made_grads, sems):
    section, place, near = where_am_i(split)
    first, second = hidden_ref.shape[0], other_hidden_ref.shape[0]
    arriving = fetch(
        [
            (hidden_ref, held_hidden.at[pl.ds(0, first)]),
            (grad_ref, held_grad.at[pl.ds(0, first)]),
            (other_hidden_ref, held_hidden.at[pl.ds(first, second)]),
            (other_grad_ref, held_grad.at[pl.ds(first, second)]),
            (gain_ref, held_gain),
            (clips_ref, held_clips),
        ],
        sems,
    )
    wait_all(arriving)
    gain_row = held_gain[...]
    leading = section == 0

    @pl.when(leading)
    def _():
        made_acts[...] = held_hidden[...].reshape(made_acts.shape)
        fill_columns(cols_ref, held_grad[...].astype(jnp.float32), dims)

    @pl.when(jnp.logical_not(leading))
    def _():
        made_grads[...] = held_grad[...].reshape(made_grads.shape)
        fill_columns(cols_ref, activate(held_hidden[...].astype(jnp.float32), gain_row).astype(jnp.float32), dims)

    def run(at, part):
        halves = (near_ref, far_ref) if part == 0 else (far_ref, near_ref)
        conv = half_spread if at == 0 else half_forward
        total = conv(cols_ref, halves[0], dims, 0) + conv(cols_ref, halves[1], dims, 1)
        if at == 0:
            ordered = take_clips(plan_ref, held_clips, dims)
            upstream = held_grad[...].astype(jnp.float32)
            back_out = back(ordered, upstream, total, gain_row).astype(jnp.bfloat16)
            made_grads[...] = back_out.reshape(made_grads.shape)
        else:
            hidden = held_hidden[...].astype(jnp.float32)
            made_acts[...] = (hidden + total).astype(jnp.bfloat16).reshape(made_acts.shape)

    on_half(section, near, run)
    wait_all(fetch([(made_acts, acts_ref), (made_grads, grads_ref)], sems))


def swap(value, axis, by):
    return lax.ppermute(value, axis, [(i, i ^ by) for i in range(lax.axis_size(axis))])


def widen(value):
    return value.astype(jnp.float32)


def narrow(value):
    return value.astype(jnp.bfloat16)


def together(*values):
    return lax.optimization_barrier(values)


def on_device(clips, plan, gains, weights, cotangent):
    peers = lax.axis_size("fsdp")
    micro, frames, height, width, channels = clips.shape
    dims = clips.shape
    voxels = frames * height * width
    total = micro * voxels
    rows = weights.shape[1]
    all_rows = rows * peers
    half_rows = all_rows // 2
    factor = 1.0 / math.sqrt(peers * total)
    order = plan[0]
    flat_clips = clips.reshape(micro, voxels, channels)
    flat_cotangent = cotangent.reshape(micro, voxels, channels)
    split = peers == 16 and rows % ROW_TILE == 0

    smem = pl.BlockSpec(memory_space=pltpu.SMEM)
    vmem = pl.BlockSpec(memory_space=pltpu.VMEM)
    anywhere = pl.BlockSpec(memory_space=pl.ANY)
    half_weight = pltpu.VMEM((half_rows, channels), jnp.bfloat16)
    clips_scratch = pltpu.VMEM((micro, voxels, channels), jnp.bfloat16)
    volume_scratch = pltpu.VMEM((total, channels), jnp.bfloat16)
    gain_scratch = pltpu.VMEM((1, channels), jnp.float32)
    cols_shape = (micro, voxels + 2 * height * width, 9 * channels)
    volume = jax.ShapeDtypeStruct((total, channels), jnp.bfloat16)
    cols_out = jax.ShapeDtypeStruct(cols_shape, jnp.bfloat16)
    half_out = jax.ShapeDtypeStruct((half_rows, channels), jnp.bfloat16)
    token_out = jax.ShapeDtypeStruct((8, 128), jnp.float32)

    def call(kernel, share, *, limit=VMEM_LIMIT, **config):
        flops = int(2 * total * all_rows * channels * share)
        return pl.pallas_call(
            functools.partial(kernel, dims, split),
            compiler_params=pltpu.CompilerParams(vmem_limit_bytes=limit),
            cost_estimate=pl.CostEstimate(flops=flops, bytes_accessed=2 * all_rows * channels, transcendentals=0),
            **config,
        )

    own = weights[0]
    signal = gains
    if split:
        held = {0: own}
        held[2] = swap(own, "fsdp", 2)
        held[4] = swap(own, "fsdp", 4)
        held[8] = swap(own, "fsdp", 8)
        signal = held[4]

    early_cols, token = call(
        prepare_kernel,
        0.2,
        out_shape=[cols_out, token_out],
        in_specs=[smem] + [vmem] * 3 + [anywhere],
        out_specs=[vmem] * 2,
    )(order, flat_clips, flat_cotangent, gains, gains)

    if split:
        held[4], token = together(held[4], token)
        held[6] = swap(held[4], "fsdp", 2)
        held[12] = swap(held[8], "fsdp", 4)
        held[10] = swap(held[8], "fsdp", 2)
        held[14] = swap(held[12], "fsdp", 2)
        for by in (0, 2, 4, 6):
            held[by + 1] = swap(held[by], "fsdp", 1)
        near = [held[by] for by in range(8)]
    else:
        full = lax.all_gather(own, "fsdp", axis=0, tiled=True)
        near, far = [full[:half_rows]], [full[half_rows:]]
    count = len(near)

    base, token, near_weight = call(
        lambda dims, split, *refs: near_kernel(dims, split, count, *refs),
        0.5,
        out_shape=[jax.ShapeDtypeStruct((total, channels), jnp.float32), token_out, half_out],
        in_specs=[vmem] * (2 + count),
        out_specs=[vmem] * 2 + [anywhere],
        scratch_shapes=[half_weight, pltpu.SemaphoreType.DMA((1,))],
    )(early_cols, token, *near)

    if split:
        held[14], token = together(held[14], token)
        for by in (8, 10, 12, 14):
            held[by + 1] = swap(held[by], "fsdp", 1)
        far = [held[by] for by in range(8, 16)]

    first_rows = micro // 2 * voxels
    mine, far_weight = call(
        lambda dims, split, *refs: far_kernel(dims, split, count, *refs),
        0.25,
        out_shape=[jax.ShapeDtypeStruct((first_rows + ROW_TILE, channels), jnp.bfloat16), half_out],
        in_specs=[smem] + [anywhere] * 3 + [vmem] * (2 + count),
        out_specs=[vmem] * 2,
        scratch_shapes=[clips_scratch, gain_scratch, pltpu.SemaphoreType.DMA((2,))],
    )(order, flat_clips, gains, token, early_cols, base, *far)
    theirs = swap(mine, "section", 1)

    other_mine = call(
        other_kernel,
        0.25,
        out_shape=jax.ShapeDtypeStruct((total - first_rows, channels), jnp.bfloat16),
        in_specs=[smem] + [anywhere] + [vmem] * 3,
        out_specs=vmem,
        scratch_shapes=[clips_scratch, pltpu.SemaphoreType.DMA((1,))],
    )(order, flat_clips, early_cols, base, far_weight)
    other_theirs = swap(other_mine, "section", 1)

    shapes = [jax.ShapeDtypeStruct((2, rows, channels), jnp.bfloat16)] * 4 if split else [half_out]
    fetched = [clips_scratch, clips_scratch, gain_scratch, pltpu.SemaphoreType.DMA((3,))]

    def operand_shapes(clip_count):
        part_rows = clip_count * voxels
        part = jax.ShapeDtypeStruct((part_rows, channels), jnp.bfloat16)
        turned_part = jax.ShapeDtypeStruct((channels, part_rows), jnp.bfloat16)
        return [part, part, turned_part, jax.ShapeDtypeStruct((clip_count, *cols_shape[1:]), jnp.bfloat16)]

    grad, hidden, first_turned, first_cols = call(
        begin_kernel,
        0.1,
        out_shape=operand_shapes(micro // 2),
        in_specs=[smem] + [anywhere] * 3 + [vmem] * 3,
        out_specs=[vmem] * 4,
        scratch_shapes=fetched,
    )(order, flat_clips, flat_cotangent, gains, mine, theirs, early_cols)

    other_grad, other_hidden, turned, late_cols, *far_sums = call(
        gradient_kernel,
        0.5,
        out_shape=operand_shapes(micro - micro // 2) + shapes,
        in_specs=[smem] + [anywhere] * 3 + [vmem] * 7,
        out_specs=[vmem] * (4 + len(shapes)),
        scratch_shapes=[half_weight] + fetched,
    )(order, flat_clips, flat_cotangent, gains, mine, theirs, other_mine, other_theirs, early_cols, first_turned,
      first_cols)

    if split:

        def core_sum(kept, sent):
            both = widen(kept) + widen(swap(sent, "fsdp", 1))
            return both[0], both[1]

        cut = rows // (2 * ROW_TILE) * ROW_TILE
        parts = slice(0, cut), slice(cut, rows)
        kept_12, send_12 = core_sum(*far_sums[:2])
        send_12 = [narrow(send_12[part]) for part in parts]

    near_sums = call(
        rest_kernel,
        0.5,
        out_shape=shapes,
        in_specs=[vmem] * 4,
        out_specs=[vmem] * len(shapes),
        scratch_shapes=[half_weight],
    )(first_turned, first_cols, turned, late_cols)

    if split:
        kept_8, send_8 = core_sum(*far_sums[2:])
        kept_4, send_4 = core_sum(*near_sums[:2])
        kept_0, send_0 = core_sum(*near_sums[2:])
        send_8 = [narrow(send_8[part]) for part in parts]
        side_4 = swap(narrow(send_4), "fsdp", 4)
        came_12 = [swap(value, "fsdp", 2) for value in send_12]
        came_8 = []
        for at in (0, 1):
            came_12[at], send_8[at] = together(came_12[at], send_8[at])
            came_8.append(swap(send_8[at], "fsdp", 2))
        for_8 = [narrow(kept_12[part] + widen(value)) for part, value in zip(parts, came_12)]
        from_4 = [swap(value, "fsdp", 4) for value in for_8]
        ready = [
            narrow(kept_8[part] + widen(one) + widen(two)) for part, one, two in zip(parts, came_8, from_4)
        ]
        from_8 = jnp.concatenate([swap(value, "fsdp", 8) for value in ready], axis=0)
        came_0 = swap(narrow(send_0 + widen(side_4)), "fsdp", 2)
        direct_4 = narrow(kept_4)
        from_4[0], direct_4 = together(from_4[0], direct_4)
        late = swap(direct_4, "fsdp", 4)
        weight_grad = (kept_0 + widen(came_0) + widen(late) + widen(from_8)) * factor
        grad, _ = together(grad, ready[1])
    else:
        summed = widen(jnp.concatenate([near_sums[0], far_sums[0]], axis=0))
        weight_grad = lax.psum_scatter(summed, "fsdp", scatter_dimension=0, tiled=True) * factor

    acts, grads = call(
        last_kernel,
        1.0,
        limit=LAST_VMEM_LIMIT,
        out_shape=[jax.ShapeDtypeStruct((1, *dims), jnp.bfloat16)] * 2,
        in_specs=[smem] + [anywhere] * 6 + [vmem] * 2,
        out_specs=[anywhere, anywhere],
        scratch_shapes=[
            pltpu.VMEM(cols_shape, jnp.bfloat16),
            clips_scratch,
            gain_scratch,
            volume_scratch,
            volume_scratch,
            pltpu.VMEM((1, *dims), jnp.bfloat16),
            pltpu.VMEM((1, *dims), jnp.bfloat16),
            pltpu.SemaphoreType.DMA((6,)),
        ],
    )(order, flat_clips, gains, hidden, grad, other_hidden, other_grad, near_weight, far_weight)
    return (acts, grads, weight_grad[None])


def solution(mesh):
    placed = (
        P("fsdp", None, None, None, None),
        P("fsdp", None),
        P("section", None),
        P("section", "fsdp", None),
        P("fsdp", None, None, None, None),
    )
    return jax.shard_map(
        on_device,
        mesh=mesh,
        in_specs=placed,
        out_specs=(
            P("section", "fsdp", None, None, None, None),
            P("section", "fsdp", None, None, None, None),
            P("section", "fsdp", None),
        ),
        check_vma=False,
    )
```
